256 devices in a mesh: dp: 8 (over z), vocab: 32 (over y, x, core).
Axes of the slice: x: 4, y: 4, z: 8, core: 2. Of those that a mesh axis runs over, the one named last changes fastest.
Arguments:
- hidden: bfloat16 [3584, 2048], P('dp', 'vocab'), may hold values from -48 to 48
- head_weight: bfloat16 [2048, 77824], P(None, 'vocab'), may hold values from -4 to 4
- kept_tiles: int32 [3584, 32], P('dp'), may hold values from 0 to 607, all different within a row
- kept_count: int32 [3584], P('dp'), may hold values from 1 to 32
- teacher_probs: bfloat16 [3584, 32, 128], P('dp', 'vocab'), may hold values from 9.9658966e-05 to 0.0099487305
Outputs:
- distill_loss: float32 [], replicated
- grad_hidden: bfloat16 [3584, 2048], P('dp', 'vocab')
- grad_weight: bfloat16 [2048, 77824], P('dp', 'vocab')
The draws below stay inside these ranges and needn't reach their ends.
Inputs may be any that keep to these rules, and one draw needn't show every extreme that they name: `kept_tiles`: the 32 entries of a row name different tiles.
All inputs are finite; a program needn't handle non-finite values.
Results may differ from the reference program's by a relative error of at most 0.018.
Values may be sent and summed in bfloat16 or wider, within the bound.
A program may use at most 128 MiB of HBM per device.

```python
import math
import jax
import jax.numpy as jnp
from jax import lax

D = 2048
TILE = 128
TILES_DEV = 19
ROWS = 448
ROWS_ALL = 3584
NTILES = 608
KMAX = 32
N_DP = 8
N_VOCAB = 32


def common_direction(key):
    sign_bits = jax.random.randint(jax.random.fold_in(key, 41), (D,), 0, 2)
    return (2.0 * sign_bits.astype(jnp.float32) - 1.0) / math.sqrt(D)


def column_noise(key, columns):
    noise_key = jax.random.fold_in(key, 17)

    def single_column(column):
        return jax.random.normal(jax.random.fold_in(noise_key, column), (D,))
    return jnp.clip(jax.vmap(single_column, out_axes=1)(columns), -4.0, 4.0)


def draw_head_weight(key, part):
    vocab_total = TILES_DEV * TILE * N_VOCAB
    columns = jnp.arange(vocab_total, dtype=jnp.int32)
    base_noise = column_noise(key, columns)
    direction = common_direction(key)
    key = jax.random.fold_in(key, 5)
    low_end, high_end = (0.5, 5.0)
    uniform_draw = jax.random.uniform(key, (vocab_total,))
    rising = 0.7 + 0.6 * columns.astype(jnp.float32) / vocab_total
    col_scale = jnp.exp(math.log(low_end) + uniform_draw * (math.log(high_end) - math.log(low_end))) * rising
    weight = base_noise * col_scale[None, :] / math.sqrt(D)
    shard_of = columns // (TILES_DEV * TILE)
    offset = 6.0 * (shard_of % 2).astype(jnp.float32) + 3.0 * columns.astype(jnp.float32) / vocab_total
    weight = weight + direction[:, None] * (offset / 3.0)[None, :]
    return weight.astype(jnp.bfloat16)


def draw_hidden(key, part):
    total_rows = ROWS * N_DP
    direction = common_direction(key)
    key = jax.random.fold_in(key, 6)
    position = jnp.arange(total_rows, dtype=jnp.float32) / total_rows
    row_noise = jnp.clip(jax.random.normal(jax.random.fold_in(key, 1), (total_rows, D)), -4.0, 4.0)
    low_end, high_end = (0.5, 5.0)
    rising = 0.6 + 1.2 * position
    uniform_draw = jax.random.uniform(jax.random.fold_in(key, 2), (total_rows,))
    row_scale = jnp.exp(math.log(low_end) + uniform_draw * (math.log(high_end) - math.log(low_end))) * rising
    rows_out = row_noise * row_scale[:, None] + 3.0 * direction[None, :]
    return rows_out.astype(jnp.bfloat16)


def touch_ends(drawn, rng, smallest, high):
    place = [jax.random.randint(jax.random.fold_in(rng, axis), (), 0, length) for axis, length in enumerate(drawn.shape)]
    longest = drawn.shape.index(max(drawn.shape))
    next_to = place[:longest] + [(place[longest] + 1) % drawn.shape[longest]] + place[longest + 1:]
    return drawn.at[tuple(place)].set(smallest).at[tuple(next_to)].set(high)


def steps_of(own_key, shape, cuts, smallest, top_value):
    def one(dim, shards_of):
        steps = jax.random.uniform(jax.random.fold_in(jax.random.fold_in(own_key, 6), dim), (shards_of,), jnp.float32, smallest / len(cuts), top_value / len(cuts))
        return jnp.repeat(jnp.exp(steps), shape[dim] // shards_of).reshape((-1,) + (1,) * (len(shape) - dim - 1))

    factor_of = one(*cuts[0])
    for cut in cuts[1:]:
        factor_of = factor_of * one(*cut)
    return factor_of


def picks_of(key, rows, count, top, lift):
    order = jax.random.permutation(jax.random.fold_in(key, 1), count)
    pull = order
    for power in range(3):
        pull = pull * pull // count
    pull = pull * lift // count
    chance = jax.random.randint(jax.random.fold_in(key, 2), (rows, count), 0, 4096) + pull
    fixed_rows = jax.random.permutation(jax.random.fold_in(key, 3), rows)[jnp.arange(count) % rows]
    chance = jnp.where(jnp.arange(rows)[:, None] == fixed_rows[None, :], 1 << 14, chance)
    merit = chance * count + jnp.arange(count)
    return lax.top_k(merit.astype(jnp.int32), top)[1].astype(jnp.int32)


def setup_inputs(seed: int = 0) -> dict:
    arg_keys = jax.random.split(jax.random.key(seed), 6)
    hidden = draw_hidden(jax.random.fold_in(arg_keys[5], 71), 0)
    head_weight = draw_head_weight(jax.random.fold_in(arg_keys[5], 71), 0)
    kept_tiles = picks_of(arg_keys[2], ROWS_ALL, NTILES, KMAX, 862)
    kept_count = touch_ends(jax.random.randint(arg_keys[3], (ROWS_ALL,), 1, KMAX + 1), jax.random.fold_in(arg_keys[3], 1), 1, KMAX).astype(jnp.int32)
    teacher_probs = jnp.clip(jnp.exp(math.log(0.0099487305) - 4.603446 * jax.random.uniform(arg_keys[4], (ROWS_ALL, KMAX, TILE), jnp.float32) ** steps_of(arg_keys[4], (ROWS_ALL, KMAX, TILE), ((0, 8), (1, 32)), -0.2, 0.2)), 9.965896606445312e-05, 0.0099487305).astype(jnp.bfloat16)
    return dict(hidden=hidden, head_weight=head_weight, kept_tiles=kept_tiles, kept_count=kept_count, teacher_probs=teacher_probs)


LOSS_SCALE = 1024.0


def replica_terms(hidden_rows, tile_rows, count_rows, prob_rows, head_weight):
    logits = jnp.dot(hidden_rows, head_weight, preferred_element_type=jnp.float32)
    row_peak = jnp.max(logits, axis=1)
    log_norm = row_peak + jnp.log(jnp.sum(jnp.exp(logits - row_peak[:, None]), axis=1))
    slot_total = tile_rows.shape[1]
    in_list = jnp.arange(slot_total, dtype=jnp.int32)[None, :] < count_rows[:, None]
    tile_ids = jnp.arange(TILES_DEV * N_VOCAB, dtype=jnp.int32)
    matches = ((tile_rows[:, :, None] == tile_ids[None, None, :]) & in_list[:, :, None]).astype(jnp.float32)
    probs_wide = prob_rows.astype(jnp.float32)
    target = jnp.einsum("rkn,rkc->rnc", matches, probs_wide).reshape(logits.shape)
    values = probs_wide * in_list[:, :, None]
    teacher_mass = jnp.sum(values, axis=(1, 2))
    weighted = jnp.sum(values * jnp.log(jnp.where(in_list[:, :, None], probs_wide, 1.0)), axis=(1, 2))
    cross_sum = jnp.sum(target * logits, axis=1)
    divergence = weighted / teacher_mass - jnp.log(teacher_mass) - cross_sum / teacher_mass + log_norm
    logit_grad = (LOSS_SCALE * (jnp.exp(logits - log_norm[:, None]) - target / teacher_mass[:, None])).astype(jnp.bfloat16)
    grad_rows = jnp.dot(logit_grad, head_weight.T, preferred_element_type=jnp.float32).astype(jnp.bfloat16)
    replica_grad = jnp.dot(hidden_rows.T, logit_grad, preferred_element_type=jnp.float32).astype(jnp.bfloat16)
    return jnp.sum(divergence), grad_rows, replica_grad


def reference(hidden, head_weight, kept_tiles, kept_count, teacher_probs):
    def replica_step(carried, replica):
        loss_total, weight_total = carried
        row_start = replica * ROWS
        hidden_rows = lax.dynamic_slice_in_dim(hidden, row_start, ROWS, 0)
        tile_rows = lax.dynamic_slice_in_dim(kept_tiles, row_start, ROWS, 0)
        count_rows = lax.dynamic_slice_in_dim(kept_count, row_start, ROWS, 0)
        prob_rows = lax.dynamic_slice_in_dim(teacher_probs, row_start, ROWS, 0)
        loss_part, grad_rows, replica_grad = replica_terms(hidden_rows, tile_rows, count_rows, prob_rows, head_weight)
        replica_grad = lax.optimization_barrier(replica_grad)
        return (loss_total + loss_part, weight_total + replica_grad.astype(jnp.float32)), grad_rows

    initial = (jnp.zeros((), jnp.float32), jnp.zeros((D, TILES_DEV * TILE * N_VOCAB), jnp.float32))
    (loss_total, weight_total), grad_blocks = lax.scan(replica_step, initial, jnp.arange(N_DP, dtype=jnp.int32))
    grad_hidden = grad_blocks.reshape(ROWS * N_DP, D)
    return loss_total / (ROWS * N_DP), grad_hidden, weight_total.astype(jnp.bfloat16)
```

```python
import functools

import jax
import jax.numpy as jnp
from jax import lax
from jax.experimental import pallas as pl
from jax.experimental.pallas import tpu as pltpu
from jax.sharding import PartitionSpec as P

LOSS_SCALE = 1024.0
MESH = pl.DeviceIdType.MESH
NY, NX, NC = 4, 4, 2
NV = NY * NX * NC
NZ = 8
ROWS = 448
D = 2048
BLK = D // NV
TILE = 128
VOC = 2432
TILES = VOC // TILE
SLICE = D // NZ
STREAMS = 4
SUB = SLICE // STREAMS
RG = 16
COLS = ((0, 512), (512, 512), (1024, 512), (1536, 512), (2048, 384))
F32 = jnp.float32
BF16 = jnp.bfloat16


def mod(a, n):
    return lax.rem(a + n, n)


def to_all_lanes(rows4):
    flat = jnp.concatenate([rows4[a : a + 1, :] for a in range(4)], axis=1)
    return jnp.broadcast_to(flat, (TILE, 4 * TILE)).T[:ROWS, :]


def kernel(
    ht_ref, w_hbm, tiles_ref, count_ref, probs_ref,
    loss_ref, gh_ref, gw_ref,
    w_ref, hbuf, h_ref, pbuf, logit_ref, targ_ref, g_ref, z_ref, mass_ref, ln_ref,
    stat_out, stat_in, ghs, ghr, gwp, ring, l1, l2,
    w_sem, h1s, h1r, h2s, h2r, h3s, h3r, p1s, p1r, p2s, p2r, p3s, p3r,
    st_s, st_r, gh_s, gh_r, l1s, l1r, l2s, l2r, rs, rr,
):
    me = lax.axis_index("vocab")
    z = lax.axis_index("dp")
    c = lax.rem(me, NC)
    chip = lax.div(me, NC)
    x = lax.rem(chip, NX)
    y = lax.div(chip, NX)
    turn = 1 - 2 * c

    def at(yy, xx, cc):
        return {"vocab": (yy * NX + xx) * NC + cc}

    def rcopy(src, dst, ss, sr, dev):
        return pltpu.make_async_remote_copy(
            src_ref=src, dst_ref=dst, send_sem=ss, recv_sem=sr, device_id=dev, device_id_type=MESH
        )

    def got(ref, sem):
        rcopy(ref, ref, sem, sem, at(y, x, 1 - c)).wait_recv()

    def sent(ref, sem):
        rcopy(ref, ref, sem, sem, at(y, x, 1 - c)).wait_send()

    w_copy = pltpu.make_async_copy(w_hbm, w_ref, w_sem)
    w_copy.start()

    barrier = pltpu.get_barrier_semaphore()

    @pl.loop(1, NV)
    def _(d):
        pl.semaphore_signal(
            barrier, inc=1, device_id={"vocab": mod(me + d, NV)}, device_id_type=MESH
        )

    @pl.loop(1, NZ)
    def _(d):
        pl.semaphore_signal(barrier, inc=1, device_id={"dp": mod(z + d, NZ)}, device_id_type=MESH)

    hbuf[y, x, c] = ht_ref[...]
    pbuf[y, x, c] = probs_ref[...]
    pl.semaphore_wait(barrier, NV - 1 + NZ - 1)

    for d in range(1, 4):
        mine = hbuf.at[y, x, c]
        rcopy(mine, mine, h1s.at[d - 1], h1r.at[d - 1], at(y, mod(x + d, NX), c)).start()
    for d in range(1, 4):
        mine = pbuf.at[y, x, c]
        rcopy(mine, mine, p1s.at[d - 1], p1r.at[d - 1], at(mod(y + d, NY), x, c)).start()

    first = me * TILES
    local = tiles_ref[...] - first
    local = jnp.where((local >= 0) & (local < TILES), local, 32)
    listed = lax.broadcasted_iota(jnp.int32, (NV, ROWS), 0) < count_ref[...]
    local = jnp.where(listed, local, -1).astype(F32).astype(BF16)
    spread = (
        lax.shift_right_logical(lax.broadcasted_iota(jnp.int32, (NV, NV * RG), 1), 4)
        == lax.broadcasted_iota(jnp.int32, (NV, NV * RG), 0)
    )
    z_ref[...] = lax.dot_general(
        local, jnp.where(spread, 1.0, 0.0).astype(BF16), (((0,), (0,)), ((), ())),
        preferred_element_type=F32,
    )

    for d in range(1, 4):
        got(hbuf.at[y, mod(x - d, NX), c], h1r.at[d - 1])

    def hrow(yy):
        return hbuf.at[yy, :, c]

    def hrow_other(yy):
        return hbuf.at[yy, :, 1 - c]

    def pcol(xx):
        return pbuf.at[:, xx, c]

    def pcol_other(xx):
        return pbuf.at[:, xx, 1 - c]

    def hsend(yy, s, to):
        rcopy(hrow(yy), hrow(yy), h2s.at[s], h2r.at[s], at(to, x, c)).start()

    def hsib(yy, s):
        rcopy(hrow(yy), hrow(yy), h3s.at[s], h3r.at[s], at(y, x, 1 - c)).start()

    def psend(xx, s, to):
        rcopy(pcol(xx), pcol(xx), p2s.at[s], p2r.at[s], at(y, to, c)).start()

    def psib(xx, s):
        rcopy(pcol(xx), pcol(xx), p3s.at[s], p3r.at[s], at(y, x, 1 - c)).start()

    hsend(y, 0, mod(y + 1, NY))
    hsend(y, 1, mod(y - 1, NY))
    hsib(y, 0)

    for d in range(1, 4):
        got(pbuf.at[mod(y - d, NY), x, c], p1r.at[d - 1])
    psend(x, 0, mod(x + 1, NX))
    psend(x, 1, mod(x - 1, NX))
    psib(x, 0)

    y_from, y_to, y_far = mod(y - turn, NY), mod(y + turn, NY), mod(y + 2, NY)
    got(hrow(y_from), h2r.at[c])
    hsend(y_from, 2, y_to)
    hsib(y_from, 1)
    got(hrow(y_to), h2r.at[1 - c])
    hsib(y_to, 2)
    got(hrow(y_far), h2r.at[2])
    hsib(y_far, 3)
    got(hrow_other(y), h3r.at[0])
    got(hrow_other(y_to), h3r.at[1])
    got(hrow_other(y_from), h3r.at[2])
    got(hrow_other(y_far), h3r.at[3])

    for i in range(NV // 2):
        pair = hbuf[i // NX, i % NX].reshape(2 * BLK, ROWS)
        h_ref[:, i * 2 * BLK : (i + 1) * 2 * BLK] = pair.T
    w_copy.wait()

    x_from, x_to, x_far = mod(x - turn, NX), mod(x + turn, NX), mod(x + 2, NX)
    peak = jnp.full((ROWS, TILE), -jnp.inf, F32)
    for n, (lo, width) in enumerate(COLS):
        part = jnp.dot(h_ref[...], w_ref[:, lo : lo + width], preferred_element_type=F32)
        logit_ref[:, lo : lo + width] = part
        for t in range(width // TILE):
            peak = jnp.maximum(peak, part[:, t * TILE : (t + 1) * TILE])
        if n == 1:
            got(pcol(x_from), p2r.at[c])
            psend(x_from, 2, x_to)
            psib(x_from, 1)
            got(pcol(x_to), p2r.at[1 - c])
            psib(x_to, 2)
    peak = jnp.max(peak, axis=1, keepdims=True)
    mass = jnp.zeros((ROWS, TILE), F32)
    for t in range(TILES):
        mass = mass + jnp.exp(logit_ref[:, t * TILE : (t + 1) * TILE] - peak)
    mass = jnp.sum(mass, axis=1, keepdims=True)

    lane = lax.broadcasted_iota(jnp.int32, (ROWS, TILE), 1)
    packed = jnp.where(lane == 0, peak, jnp.where(lane == 1, mass, 0.0))
    packed = jnp.concatenate([packed, jnp.zeros((4 * TILE - ROWS, TILE), F32)], axis=0).T
    message = jnp.concatenate(
        [packed[i : i + 1, a * TILE : (a + 1) * TILE] for i in range(2) for a in range(4)], axis=0
    )
    stat_out[...] = message
    stat_in[me] = message

    @pl.loop(1, NV)
    def _(d):
        rcopy(stat_out, stat_in.at[me], st_s, st_r, {"vocab": mod(me + d, NV)}).start()

    got(pcol(x_far), p2r.at[2])
    psib(x_far, 3)
    got(pcol_other(x), p3r.at[0])
    got(pcol_other(x_to), p3r.at[1])
    got(pcol_other(x_from), p3r.at[2])
    got(pcol_other(x_far), p3r.at[3])

    own = lax.rem(lax.broadcasted_iota(jnp.int32, (RG, NV * RG), 1), RG) == (
        lax.broadcasted_iota(jnp.int32, (RG, NV * RG), 0)
    )

    @pl.loop(0, ROWS // RG)
    def _(g):
        rows = pl.ds(pl.multiple_of(g * RG, RG), RG)
        place = jnp.where(own, z_ref[rows, :], -1.0)
        blocks = [jnp.where(place == float(n), 1.0, 0.0).astype(BF16) for n in range(TILES)]
        blocks.append(jnp.where(place >= 0.0, 1.0, 0.0).astype(BF16))
        entries = pbuf[:, :, :, rows, :].reshape(NV * RG, TILE)
        placed = jnp.dot(jnp.concatenate(blocks, axis=0), entries, preferred_element_type=F32)
        for n in range(TILES):
            targ_ref[rows, n * TILE : (n + 1) * TILE] = placed[n * RG : (n + 1) * RG].astype(BF16)
        mass_ref[rows, :] = placed[TILES * RG :]

    teacher = jnp.sum(mass_ref[...], axis=1, keepdims=True)
    scale = 1.0 / teacher
    mass_ref[...] = jnp.broadcast_to(LOSS_SCALE * scale, (ROWS, TILE))
    cross = jnp.zeros((ROWS, TILE), F32)
    for t in range(TILES):
        cols = slice(t * TILE, (t + 1) * TILE)
        cross = cross + targ_ref[:, cols].astype(F32) * logit_ref[:, cols]
    entries = probs_ref[...].astype(F32)
    counts = jnp.broadcast_to(count_ref[...].astype(F32), (TILE, ROWS)).T
    weighted = jnp.where(counts > me.astype(F32), entries * jnp.log(entries), 0.0)
    shares = jnp.sum((weighted - cross) * scale)

    got(stat_in.at[pl.ds(0, NV - 1)], st_r)
    stats = stat_in[...]
    peaks, masses = stats[:, 0:4, :], stats[:, 4:8, :]
    top = jnp.max(peaks, axis=0)
    real = (
        lax.broadcasted_iota(jnp.int32, (4, TILE), 0) * TILE
        + lax.broadcasted_iota(jnp.int32, (4, TILE), 1)
    ) < ROWS
    total = jnp.where(real, jnp.sum(masses * jnp.exp(peaks - top[None]), axis=0), 1.0)
    log_norm = top + jnp.log(total)
    ln_ref[...] = to_all_lanes(log_norm)

    @pl.loop(0, TILES)
    def _(t):
        cols = pl.ds(pl.multiple_of(t * TILE, TILE), TILE)
        soft = LOSS_SCALE * jnp.exp(logit_ref[:, cols] - ln_ref[...])
        g_ref[:, cols] = (soft - targ_ref[:, cols].astype(F32) * mass_ref[...]).astype(BF16)

    def head_block(j):
        quarter = hbuf[lax.div(j, 2), pl.ds(2 * lax.rem(j, 2), 2)].reshape(SLICE, ROWS)
        for lo, width in COLS:
            gwp[j, :, lo : lo + width] = jnp.dot(
                quarter, g_ref[:, lo : lo + width], preferred_element_type=F32
            ).astype(BF16)

    def stream_rows(q):
        return pl.ds(q * SUB, SUB)

    def ahead(q):
        return 1 if q < STREAMS // 2 else -1

    def ring_send(q, src, step):
        rcopy(
            src, ring.at[q, step], rs.at[q, step], rr.at[q, step],
            {"dp": mod(z + ahead(q), NZ)},
        ).start()

    for way in (1, -1):
        j = mod(z - way, NZ)
        head_block(j)
        for q in range(STREAMS):
            if ahead(q) == way:
                ring_send(q, gwp.at[j, stream_rows(q)], 0)

    @pl.loop(0, 4)
    def _(i):
        rows = pl.ds(pl.multiple_of(i * 512, 512), 512)
        part = lax.dot_general(
            w_ref[rows, :], g_ref[...], (((1,), (1,)), ((), ())), preferred_element_type=F32
        )
        ghs[pl.ds(i * 8, 8)] = part.astype(BF16).reshape(8, BLK, ROWS)

    ghr[me] = ghs[me]

    @pl.loop(1, NV)
    def _(d):
        to = mod(me + d, NV)
        rcopy(ghs.at[to], ghr.at[me], gh_s, gh_r, {"vocab": to}).start()

    mass_col = jnp.log(teacher)
    common = jnp.sum(ln_ref[:, 0:1] - mass_col) * (1.0 / NV)
    l1[me] = jnp.broadcast_to(shares + common, (8, TILE))

    @pl.loop(1, NV)
    def _(d):
        rcopy(l1.at[me], l1.at[me], l1s, l1r, {"vocab": mod(me + d, NV)}).start()

    @pl.loop(2, NZ - 1)
    def _(i):
        head_block(mod(z + i, NZ))

    head_block(z)

    def ring_step(q, step):
        got(ring.at[q, step], rr.at[q, step])
        j = mod(z - ahead(q) * (2 + step) + NZ, NZ)
        both = ring[q, step].astype(F32) + gwp[j, q * SUB : (q + 1) * SUB, :].astype(F32)
        if step == NZ - 2:
            gw_ref[q * SUB : (q + 1) * SUB, :] = both.astype(BF16)
        else:
            ring[q, step] = both.astype(BF16)
            ring_send(q, ring.at[q, step], step + 1)

    order = (0, 2, 1, 3)
    for step in range(NZ - 1):
        for q in order:
            ring_step(q, step)
        if step == 1:
            got(l1.at[pl.ds(0, NV - 1)], l1r)
            l2[z] = jnp.sum(l1[...], axis=0)

            @pl.loop(1, NZ)
            def _(d):
                rcopy(l2.at[z], l2.at[z], l2s, l2r, {"dp": mod(z + d, NZ)}).start()

        if step == 3:
            got(ghr.at[pl.ds(0, NV - 1)], gh_r)
            total = jnp.zeros((BLK, ROWS), F32)
            for i in range(NV):
                total = total + ghr[i].astype(F32)
            gh_ref[...] = total.astype(BF16)
            got(l2.at[pl.ds(0, NZ - 1)], l2r)
            loss_ref[...] = jnp.sum(l2[...], axis=0) * (1.0 / (ROWS * NZ))

    for d in range(3):
        sent(hbuf.at[y, x, c], h1s.at[d])
        sent(pbuf.at[y, x, c], p1s.at[d])
        sent(hrow(y), h2s.at[d])
        sent(pcol(x), p2s.at[d])
    for d in range(4):
        sent(hrow(y), h3s.at[d])
        sent(pcol(x), p3s.at[d])
    sent(stat_in.at[pl.ds(0, NV - 1)], st_s)
    sent(ghr.at[pl.ds(0, NV - 1)], gh_s)
    sent(l1.at[pl.ds(0, NV - 1)], l1s)
    sent(l2.at[pl.ds(0, NZ - 1)], l2s)
    for q in range(STREAMS):
        for step in range(NZ - 1):
            sent(ring.at[q, step], rs.at[q, step])


def shards(hidden, head_weight, kept_tiles, kept_count, teacher_probs):
    vmem = pl.BlockSpec(memory_space=pltpu.VMEM)
    dma = pltpu.SemaphoreType.DMA
    loss, gh, gw = pl.pallas_call(
        kernel,
        out_shape=(
            jax.ShapeDtypeStruct((8, TILE), F32),
            jax.ShapeDtypeStruct((BLK, ROWS), BF16),
            jax.ShapeDtypeStruct((SLICE, VOC), BF16),
        ),
        in_specs=[vmem, pl.BlockSpec(memory_space=pl.ANY), vmem, vmem, vmem],
        out_specs=(vmem, vmem, vmem),
        scratch_shapes=[
            pltpu.VMEM((D, VOC), BF16),
            pltpu.VMEM((NY, NX, NC, BLK, ROWS), BF16),
            pltpu.VMEM((ROWS, D), BF16),
            pltpu.VMEM((NY, NX, NC, ROWS, TILE), BF16),
            pltpu.VMEM((ROWS, VOC), F32),
            pltpu.VMEM((ROWS, VOC), BF16),
            pltpu.VMEM((ROWS, VOC), BF16),
            pltpu.VMEM((ROWS, NV * RG), F32),
            pltpu.VMEM((ROWS, TILE), F32),
            pltpu.VMEM((ROWS, TILE), F32),
            pltpu.VMEM((8, TILE), F32),
            pltpu.VMEM((NV, 8, TILE), F32),
            pltpu.VMEM((NV, BLK, ROWS), BF16),
            pltpu.VMEM((NV, BLK, ROWS), BF16),
            pltpu.VMEM((NZ, SLICE, VOC), BF16),
            pltpu.VMEM((STREAMS, NZ - 1, SUB, VOC), BF16),
            pltpu.VMEM((NV, 8, TILE), F32),
            pltpu.VMEM((NZ, 8, TILE), F32),
            dma,
            dma((3,)), dma((3,)), dma((3,)), dma((3,)), dma((4,)), dma((4,)),
            dma((3,)), dma((3,)), dma((3,)), dma((3,)), dma((4,)), dma((4,)),
            dma, dma, dma, dma, dma, dma, dma, dma,
            dma((STREAMS, NZ - 1)), dma((STREAMS, NZ - 1)),
        ],
        compiler_params=pltpu.CompilerParams(
            collective_id=0, has_side_effects=True, vmem_limit_bytes=58 * 1024 * 1024
        ),
        cost_estimate=pl.CostEstimate(
            flops=6 * ROWS * D * VOC, bytes_accessed=2 * D * VOC, transcendentals=2 * ROWS * VOC
        ),
    )(
        hidden.T,
        head_weight,
        kept_tiles.T,
        kept_count.reshape(1, ROWS),
        teacher_probs.reshape(ROWS, TILE),
    )
    return loss[0, 0], gh.T, gw


def solution(mesh):
    return jax.shard_map(
        shards,
        mesh=mesh,
        in_specs=(
            P("dp", "vocab"),
            P(None, "vocab"),
            P("dp", None),
            P("dp"),
            P("dp", "vocab", None),
        ),
        out_specs=(P(), P("dp", "vocab"), P("dp", "vocab")),
        check_vma=False,
    )
```

```python
import jax
import jax.numpy as jnp
from jax import lax
from jax.experimental import pallas as pl
from jax.experimental.pallas import tpu as pltpu
from jax.sharding import PartitionSpec as P

LOSS_SCALE = 1024.0
MESH = pl.DeviceIdType.MESH
NS = 4
NC = 2
NV = NS * NS * NC
NZ = 8
ROWS = 448
D = 2048
BLK = D // NV
TILE = 128
VOC = 2432
TILES = VOC // TILE
SLOTS = 3
WIDE = SLOTS * TILE
SLICE = D // NZ
RG = 16
COLS = ((0, 512), (512, 512), (1024, 512), (1536, 512), (2048, 384))
F32 = jnp.float32
BF16 = jnp.bfloat16


def mod(a, n):
    return lax.rem(a + n, n)


def flat_row(rows4):
    return jnp.concatenate([rows4[a : a + 1, :] for a in range(4)], axis=1)


def to_all_lanes(rows4):
    return jnp.broadcast_to(flat_row(rows4), (TILE, 4 * TILE)).T[:ROWS, :]


def tile_cols(t):
    return pl.ds(pl.multiple_of(t * TILE, TILE), TILE)


def kernel(
    ht_ref, w_hbm, tiles_ref, count_ref, probs_ref,
    loss_ref, gh_ref, gw_ref,
    w_ref, hall, h_ref, pbuf, logit_ref, targ_ref, g_ref, z_ref, mass_ref, ln_ref,
    wt_ref, t_in, grad_ref, gws, stat_out, stat_in, stat_z, ghs, ghr, l1, l2,
    w_sem, zhs, zhr, h_sems, p_sems, o_sems,
    st_s, st_r, gh_s, gh_r, l1s, l1r, l2s, l2r, sz_s, sz_r, ts, tr, ts2, tr2, ws, wr, ws2, wr2,
):
    me = lax.axis_index("vocab")
    z = lax.axis_index("dp")
    c = lax.rem(me, NC)
    chip = lax.div(me, NC)
    x = lax.rem(chip, NS)
    y = lax.div(chip, NS)
    a = x + c * (y - x)
    b = y + c * (x - y)

    def place(cc, bb, aa):
        yy = bb + cc * (aa - bb)
        xx = aa + cc * (bb - aa)
        return {"vocab": (yy * NS + xx) * NC + cc}

    sibling = {"vocab": chip * NC + 1 - c}

    def at_z(zz):
        return {"dp": zz}

    def owns3(zz):
        return lax.rem(zz, 3) == 0

    def tile_of(zz, s):
        return 16 + lax.div(zz, 3) if s == 2 else zz + 8 * s

    def rcopy(src, dst, ss, sr, dev):
        return pltpu.make_async_remote_copy(
            src_ref=src, dst_ref=dst, send_sem=ss, recv_sem=sr, device_id=dev, device_id_type=MESH
        )

    def got(ref, sem):
        rcopy(ref, ref, sem, sem, sibling).wait_recv()

    def sent(ref, sem):
        rcopy(ref, ref, sem, sem, sibling).wait_send()

    class Gather:
        def __init__(self, block, line, half, sems):
            self.block, self.line, self.half = block, line, half
            self.s, self.r = sems

        def first(self):
            for d in range(1, NS):
                ref = self.block(c, b, a)
                to = place(c, b, mod(a + d, NS))
                rcopy(ref, ref, self.s.at[d - 1], self.r.at[d - 1], to).start()

        def _side(self, bb, i):
            ref = self.line(c, bb)
            rcopy(ref, ref, self.s.at[7 + i], self.r.at[7 + i], sibling).start()

        def second(self):
            for d in range(1, NS):
                got(self.block(c, b, mod(a - d, NS)), self.r.at[d - 1])
            ref = self.line(c, b)
            for i, d in enumerate((1, -1)):
                rcopy(ref, ref, self.s.at[3 + i], self.r.at[3 + i], place(c, mod(b + d, NS), a)).start()
            self._side(b, 0)

        def relay(self):
            for i, d in enumerate((1, -1)):
                bb = mod(b - d, NS)
                got(self.line(c, bb), self.r.at[3 + i])
                ref = self.half(c, bb, i)
                rcopy(ref, ref, self.s.at[5 + i], self.r.at[5 + i], place(c, mod(b + d, NS), a)).start()
                self._side(bb, 1 + i)

        def last(self):
            bb = mod(b + 2, NS)
            for i in range(2):
                got(self.half(c, bb, i), self.r.at[5 + i])
            self._side(bb, 3)

        def finish(self):
            for i, d in enumerate((0, -1, 1, 2)):
                got(self.line(1 - c, mod(a + d, NS)), self.r.at[7 + i])

        def drain(self):
            for i in range(3):
                sent(self.block(c, b, a), self.s.at[i])
            for i in range(2):
                sent(self.line(c, b), self.s.at[3 + i])
                sent(self.half(c, b, i), self.s.at[5 + i])
            for i in range(4):
                sent(self.line(c, b), self.s.at[7 + i])

    own_h = Gather(
        lambda cc, bb, aa: hall.at[cc, bb, aa, 0],
        lambda cc, bb: hall.at[cc, bb, :, 0],
        lambda cc, bb, i: hall.at[cc, bb, pl.ds(2 * i, 2), 0],
        h_sems,
    )
    probs = Gather(
        lambda cc, bb, aa: pbuf.at[cc, bb, aa],
        lambda cc, bb: pbuf.at[cc, bb],
        lambda cc, bb, i: pbuf.at[cc, bb, pl.ds(2 * i, 2)],
        p_sems,
    )
    others = pl.ds(1, NZ - 1)
    other_h = Gather(
        lambda cc, bb, aa: hall.at[cc, bb, aa, others],
        lambda cc, bb: hall.at[cc, bb, :, others],
        lambda cc, bb, i: hall.at[cc, bb, pl.ds(2 * i, 2), others],
        o_sems,
    )

    w_copy = pltpu.make_async_copy(w_hbm, w_ref, w_sem)
    w_copy.start()

    barrier = pltpu.get_barrier_semaphore()

    @pl.loop(1, NV)
    def _(d):
        pl.semaphore_signal(
            barrier, inc=1, device_id={"vocab": mod(me + d, NV)}, device_id_type=MESH
        )

    @pl.loop(1, NZ)
    def _(d):
        pl.semaphore_signal(barrier, inc=1, device_id=at_z(mod(z + d, NZ)), device_id_type=MESH)

    hall[c, b, a, 0] = ht_ref[...]
    pbuf[c, b, a] = probs_ref[...]

    local = tiles_ref[...] - me * TILES
    local = jnp.where((local >= 0) & (local < TILES), local, 32)
    listed = lax.broadcasted_iota(jnp.int32, (NV, ROWS), 0) < count_ref[...]
    local = jnp.where(listed, local, -1).astype(F32).astype(BF16)
    slot = lax.shift_right_logical(lax.broadcasted_iota(jnp.int32, (NV, NV * RG), 1), 4)
    slot_b = lax.shift_right_logical(slot, 2) & 3
    slot_a = slot & 3
    position = jnp.where(slot < 16, slot_b * 8 + slot_a * 2, slot_a * 8 + slot_b * 2 + 1)
    spread = position == lax.broadcasted_iota(jnp.int32, (NV, NV * RG), 0)
    z_ref[...] = lax.dot_general(
        local, jnp.where(spread, 1.0, 0.0).astype(BF16), (((0,), (0,)), ((), ())),
        preferred_element_type=F32,
    )

    @pl.when(jnp.logical_not(owns3(z)))
    def _():
        for d in range(NZ):
            t_in[d, 2] = jnp.zeros((ROWS, TILE), BF16)

    pl.semaphore_wait(barrier, NV - 1 + NZ - 1)

    probs.first()
    own_h.first()
    for d in range(1, NZ):
        rcopy(
            hall.at[c, b, a, 0], hall.at[c, b, a, NZ - d], zhs.at[d - 1], zhr.at[d - 1],
            at_z(mod(z + d, NZ)),
        ).start()
    probs.second()
    own_h.second()

    w_copy.wait()
    for s in range(SLOTS):
        cols = tile_cols(tile_of(z, s))
        pieces = []
        for i in range(NV):
            cc, bb, aa = i // 16, i // 4 % 4, i % 4
            v = (bb * NS + aa) * NC if cc == 0 else (aa * NS + bb) * NC + 1
            pieces.append(w_ref[v * BLK : (v + 1) * BLK, cols])
        wt_ref[s * TILE : (s + 1) * TILE, :] = jnp.concatenate(pieces, axis=0).T

    probs.relay()
    own_h.relay()
    for d in range(1, NZ):
        got(hall.at[c, b, a, NZ - d], zhr.at[d - 1])
    other_h.first()
    probs.last()
    probs.finish()

    own = lax.rem(lax.broadcasted_iota(jnp.int32, (RG, NV * RG), 1), RG) == (
        lax.broadcasted_iota(jnp.int32, (RG, NV * RG), 0)
    )

    @pl.loop(0, ROWS // RG)
    def _(g):
        rows = pl.ds(pl.multiple_of(g * RG, RG), RG)
        spot = jnp.where(own, z_ref[rows, :], -1.0)
        blocks = [jnp.where(spot == float(n), 1.0, 0.0).astype(BF16) for n in range(TILES)]
        blocks.append(jnp.where(spot >= 0.0, 1.0, 0.0).astype(BF16))
        entries = pbuf[:, :, :, rows, :].reshape(NV * RG, TILE)
        placed = jnp.dot(jnp.concatenate(blocks, axis=0), entries, preferred_element_type=F32)
        for n in range(TILES):
            targ_ref[n, rows, :] = placed[n * RG : (n + 1) * RG].astype(BF16)
        mass_ref[rows, :] = placed[TILES * RG :]

    for d in range(1, NZ):
        to = mod(z + d, NZ)
        for s in range(2):
            rcopy(targ_ref.at[tile_of(to, s)], t_in.at[NZ - d, s], ts, tr, at_z(to)).start()

        @pl.when(owns3(to))
        def _():
            rcopy(targ_ref.at[tile_of(to, 2)], t_in.at[NZ - d, 2], ts2.at[d], tr2, at_z(to)).start()

    for s in range(2):
        t_in[0, s] = targ_ref[tile_of(z, s)]

    @pl.when(owns3(z))
    def _():
        t_in[0, 2] = targ_ref[tile_of(z, 2)]

    own_h.last()
    own_h.finish()
    other_h.second()
    for i in range(NV // 2):
        yy, xx = i // NS, i % NS
        pair = jnp.concatenate([hall[0, yy, xx, 0], hall[1, xx, yy, 0]], axis=0)
        h_ref[:, i * 2 * BLK : (i + 1) * 2 * BLK] = pair.T

    peak = jnp.full((ROWS, TILE), -jnp.inf, F32)
    for lo, width in COLS:
        part = jnp.dot(h_ref[...], w_ref[:, lo : lo + width], preferred_element_type=F32)
        for t in range(width // TILE):
            one = part[:, t * TILE : (t + 1) * TILE]
            logit_ref[lo // TILE + t] = one
            peak = jnp.maximum(peak, one)
    peak = jnp.max(peak, axis=1, keepdims=True)
    mass = jnp.zeros((ROWS, TILE), F32)
    for t in range(TILES):
        mass = mass + jnp.exp(logit_ref[t] - peak)
    mass = jnp.sum(mass, axis=1, keepdims=True)

    lane = lax.broadcasted_iota(jnp.int32, (ROWS, TILE), 1)

    def message_of(first, second):
        packed = jnp.where(lane == 0, first, jnp.where(lane == 1, second, 0.0))
        packed = jnp.concatenate([packed, jnp.zeros((4 * TILE - ROWS, TILE), F32)], axis=0).T
        return jnp.concatenate(
            [packed[i : i + 1, k * TILE : (k + 1) * TILE] for i in range(2) for k in range(4)],
            axis=0,
        )

    message = message_of(peak, mass)
    stat_out[...] = message
    stat_in[me] = message

    @pl.loop(1, NV)
    def _(d):
        rcopy(stat_out, stat_in.at[me], st_s, st_r, {"vocab": mod(me + d, NV)}).start()

    teacher = jnp.sum(mass_ref[...], axis=1, keepdims=True)
    scale = 1.0 / teacher
    mass_ref[...] = jnp.broadcast_to(LOSS_SCALE * scale, (ROWS, TILE))
    scale_rows = message_of(LOSS_SCALE * scale, jnp.log(teacher))
    cross = jnp.zeros((ROWS, TILE), F32)
    for t in range(TILES):
        cross = cross + targ_ref[t].astype(F32) * logit_ref[t]
    entries = probs_ref[...].astype(F32)
    counts = jnp.broadcast_to(count_ref[...].astype(F32), (TILE, ROWS)).T
    weighted = jnp.where(counts > me.astype(F32), entries * jnp.log(entries), 0.0)
    shares = jnp.sum((weighted - cross) * scale)

    got(stat_in.at[pl.ds(0, NV - 1)], st_r)
    stats = stat_in[...]
    peaks, masses = stats[:, 0:4, :], stats[:, 4:8, :]
    top = jnp.max(peaks, axis=0)
    real = (
        lax.broadcasted_iota(jnp.int32, (4, TILE), 0) * TILE
        + lax.broadcasted_iota(jnp.int32, (4, TILE), 1)
    ) < ROWS
    total = jnp.where(real, jnp.sum(masses * jnp.exp(peaks - top[None]), axis=0), 1.0)
    log_norm = jnp.where(real, top + jnp.log(total), 0.0)
    stat_z[0] = jnp.concatenate([log_norm, scale_rows[0:4]], axis=0)
    for d in range(1, NZ):
        rcopy(stat_z.at[0], stat_z.at[NZ - d], sz_s, sz_r, at_z(mod(z + d, NZ))).start()
    ln_ref[...] = to_all_lanes(log_norm)
    common = jnp.sum(jnp.where(real, log_norm - scale_rows[4:8], 0.0)) * (1.0 / NV)
    l1[me] = jnp.broadcast_to(shares + common, (8, TILE))

    @pl.loop(1, NV)
    def _(d):
        rcopy(l1.at[me], l1.at[me], l1s, l1r, {"vocab": mod(me + d, NV)}).start()

    @pl.loop(0, TILES)
    def _(t):
        soft = LOSS_SCALE * jnp.exp(logit_ref[t] - ln_ref[...])
        g_ref[:, tile_cols(t)] = (soft - targ_ref[t].astype(F32) * mass_ref[...]).astype(BF16)

    @pl.loop(0, 4)
    def _(i):
        rows = pl.ds(pl.multiple_of(i * 512, 512), 512)
        part = lax.dot_general(
            w_ref[rows, :], g_ref[...], (((1,), (1,)), ((), ())), preferred_element_type=F32
        )
        ghs[pl.ds(i * 8, 8)] = part.astype(BF16).reshape(8, BLK, ROWS)

    ghr[me] = ghs[me]

    other_h.relay()
    other_h.last()

    @pl.loop(1, NV)
    def _(d):
        to = mod(me + d, NV)
        rcopy(ghs.at[to], ghr.at[me], gh_s, gh_r, {"vocab": to}).start()

    got(l1.at[pl.ds(0, NV - 1)], l1r)
    l2[z] = jnp.sum(l1[...], axis=0)

    @pl.loop(1, NZ)
    def _(d):
        rcopy(l2.at[z], l2.at[z], l2s, l2r, at_z(mod(z + d, NZ))).start()

    got(stat_z.at[pl.ds(0, NZ - 1)], sz_r)
    other_h.finish()

    @pl.loop(0, NZ)
    def _(d):
        rows = hall[:, :, :, d].reshape(D, ROWS)
        part = jnp.dot(wt_ref[...], rows, preferred_element_type=F32)
        norm = flat_row(stat_z[d, 0:4])[:, :ROWS]
        soft = (LOSS_SCALE * jnp.exp(part - norm)).T
        for s in range(SLOTS):
            logit_ref[d * SLOTS + s] = soft[:, s * TILE : (s + 1) * TILE]

    got(t_in.at[pl.ds(1, NZ - 1), pl.ds(0, 2)], tr)

    @pl.when(owns3(z))
    def _():
        got(t_in.at[pl.ds(1, NZ - 1), 2], tr2)

    @pl.loop(0, NZ)
    def _(d):
        mass_ref[...] = to_all_lanes(stat_z[d, 4:8])
        for s in range(SLOTS):
            grad_ref[d, :, s * TILE : (s + 1) * TILE] = (
                logit_ref[d * SLOTS + s] - t_in[d, s].astype(F32) * mass_ref[...]
            ).astype(BF16)

    def head_block(j):
        yy, xx = lax.div(j, 2), 2 * lax.rem(j, 2)
        total = jnp.zeros((SLICE, WIDE), F32)
        for d in range(NZ):
            part = [
                hall[0, yy, xx, d], hall[1, xx, yy, d], hall[0, yy, xx + 1, d], hall[1, xx + 1, yy, d]
            ]
            total = total + jnp.dot(
                jnp.concatenate(part, axis=0), grad_ref[d], preferred_element_type=F32
            )
        return total.astype(BF16)

    @pl.loop(1, NZ)
    def _(i):
        j = mod(z + i, NZ)
        done = head_block(j)
        for s in range(SLOTS):
            gws[i, s] = done[:, s * TILE : (s + 1) * TILE]
        for s in range(2):
            rcopy(gws.at[i, s], gw_ref.at[:, tile_cols(tile_of(z, s))], ws, wr, at_z(j)).start()

        @pl.when(owns3(z))
        def _():
            rcopy(
                gws.at[i, 2], gw_ref.at[:, tile_cols(tile_of(z, 2))],
                ws2, wr2.at[lax.div(z, 3)], at_z(j),
            ).start()

    done = head_block(z)
    for s in range(2):
        gw_ref[:, tile_cols(tile_of(z, s))] = done[:, s * TILE : (s + 1) * TILE]

    @pl.when(owns3(z))
    def _():
        gw_ref[:, tile_cols(tile_of(z, 2))] = done[:, 2 * TILE :]

    got(ghr.at[pl.ds(0, NV - 1)], gh_r)
    sum_h = jnp.zeros((BLK, ROWS), F32)
    for i in range(NV):
        sum_h = sum_h + ghr[i].astype(F32)
    gh_ref[...] = sum_h.astype(BF16)
    got(l2.at[pl.ds(0, NZ - 1)], l2r)
    loss_ref[...] = jnp.sum(l2[...], axis=0) * (1.0 / (ROWS * NZ))

    probs.drain()
    own_h.drain()
    other_h.drain()
    for d in range(1, NZ):
        sent(hall.at[c, b, a, 0], zhs.at[d - 1])
    sent(stat_in.at[pl.ds(0, NV - 1)], st_s)
    sent(ghr.at[pl.ds(0, NV - 1)], gh_s)
    sent(l1.at[pl.ds(0, NV - 1)], l1s)
    sent(l2.at[pl.ds(0, NZ - 1)], l2s)
    sent(stat_z.at[pl.ds(0, NZ - 1)], sz_s)
    sent(t_in.at[pl.ds(1, NZ - 1), pl.ds(0, 2)], ts)
    for d in range(1, NZ):

        @pl.when(owns3(mod(z + d, NZ)))
        def _():
            sent(targ_ref.at[0], ts2.at[d])

    sent(gws.at[pl.ds(1, NZ - 1), pl.ds(0, 2)], ws)

    @pl.when(owns3(z))
    def _():
        sent(gws.at[pl.ds(1, NZ - 1), 2], ws2)

    got(gws.at[pl.ds(1, NZ - 1), pl.ds(0, 2)], wr)
    for i in range(SLOTS):

        @pl.when(z != 3 * i)
        def _():
            got(gws.at[0, 0], wr2.at[i])


def shards(hidden, head_weight, kept_tiles, kept_count, teacher_probs):
    vmem = pl.BlockSpec(memory_space=pltpu.VMEM)
    dma = pltpu.SemaphoreType.DMA
    loss, gh, gw = pl.pallas_call(
        kernel,
        out_shape=(
            jax.ShapeDtypeStruct((8, TILE), F32),
            jax.ShapeDtypeStruct((BLK, ROWS), BF16),
            jax.ShapeDtypeStruct((SLICE, VOC), BF16),
        ),
        in_specs=[vmem, pl.BlockSpec(memory_space=pl.ANY), vmem, vmem, vmem],
        out_specs=(vmem, vmem, vmem),
        scratch_shapes=[
            pltpu.VMEM((D, VOC), BF16),
            pltpu.VMEM((NC, NS, NS, NZ, BLK, ROWS), BF16),
            pltpu.VMEM((ROWS, D), BF16),
            pltpu.VMEM((NC, NS, NS, ROWS, TILE), BF16),
            pltpu.VMEM((NZ * SLOTS, ROWS, TILE), F32),
            pltpu.VMEM((TILES, ROWS, TILE), BF16),
            pltpu.VMEM((ROWS, VOC), BF16),
            pltpu.VMEM((ROWS, NV * RG), F32),
            pltpu.VMEM((ROWS, TILE), F32),
            pltpu.VMEM((ROWS, TILE), F32),
            pltpu.VMEM((WIDE, D), BF16),
            pltpu.VMEM((NZ, SLOTS, ROWS, TILE), BF16),
            pltpu.VMEM((NZ, ROWS, WIDE), BF16),
            pltpu.VMEM((NZ, SLOTS, SLICE, TILE), BF16),
            pltpu.VMEM((8, TILE), F32),
            pltpu.VMEM((NV, 8, TILE), F32),
            pltpu.VMEM((NZ, 8, TILE), F32),
            pltpu.VMEM((NV, BLK, ROWS), BF16),
            pltpu.VMEM((NV, BLK, ROWS), BF16),
            pltpu.VMEM((NV, 8, TILE), F32),
            pltpu.VMEM((NZ, 8, TILE), F32),
            dma, dma((NZ - 1,)), dma((NZ - 1,)),
            [dma((11,)), dma((11,))], [dma((11,)), dma((11,))], [dma((11,)), dma((11,))],
            dma, dma, dma, dma, dma, dma, dma, dma, dma, dma,
            dma, dma, dma((NZ,)), dma, dma, dma, dma, dma((SLOTS,)),
        ],
        compiler_params=pltpu.CompilerParams(
            collective_id=0, has_side_effects=True, vmem_limit_bytes=60 * 1024 * 1024
        ),
        cost_estimate=pl.CostEstimate(
            flops=8 * ROWS * D * VOC, bytes_accessed=2 * D * VOC, transcendentals=3 * ROWS * VOC
        ),
    )(
        hidden.T,
        head_weight,
        kept_tiles.T,
        kept_count.reshape(1, ROWS),
        teacher_probs.reshape(ROWS, TILE),
    )
    return loss[0, 0], gh.T, gw


def solution(mesh):
    return jax.shard_map(
        shards,
        mesh=mesh,
        in_specs=(
            P("dp", "vocab"),
            P(None, "vocab"),
            P("dp", None),
            P("dp"),
            P("dp", "vocab", None),
        ),
        out_specs=(P(), P("dp", "vocab"), P("dp", "vocab")),
        check_vma=False,
    )
```

```python
import jax
import jax.numpy as jnp
from jax import lax
from jax.experimental import pallas as pl
from jax.experimental.pallas import tpu as pltpu
from jax.sharding import PartitionSpec as P

LOSS_SCALE = 1024.0
MESH = pl.DeviceIdType.MESH
NS = 4
NC = 2
NV = NS * NS * NC
NZ = 8
ROWS = 448
D = 2048
BLK = D // NV
TILE = 128
VOC = 2432
TILES = VOC // TILE
SLOTS = 3
WIDE = SLOTS * TILE
SLICE = D // NZ
RG = 16
HALF = ROWS // 2
ALL = ROWS * NZ
KEPT = 3 * TILE
STEP = 512
COLS = ((0, 512), (512, 512), (1024, 512), (1536, 512), (2048, 384))
F32 = jnp.float32
BF16 = jnp.bfloat16


def mod(a, n):
    return lax.rem(a + n, n)


def flat_row(rows4):
    return jnp.concatenate([rows4[a : a + 1, :] for a in range(4)], axis=1)


def to_all_lanes(rows4):
    return jnp.broadcast_to(flat_row(rows4), (TILE, 4 * TILE)).T[:ROWS, :]


def tile_cols(t):
    return pl.ds(pl.multiple_of(t * TILE, TILE), TILE)


def tile_rows(t):
    return slice(t * ROWS, (t + 1) * ROWS) if isinstance(t, int) else pl.ds(
        pl.multiple_of(t * ROWS, ROWS), ROWS
    )


def kernel(
    ht_ref, w_hbm, tiles_ref, count_ref, probs_ref,
    loss_ref, gh_ref, gw_ref,
    w_ref, hall, hown, zin, lnf_ref, col_ref, h_ref, pbuf, logit_ref, targ_ref, g_ref, z_ref, mass_ref, ln_ref,
    wt_ref, t_in, grad_ref, gws, stat_out, stat_in, stat_z, ghs, ghr, l1, l2,
    w_sem, zhs, zhr, h_sems, p_sems, q_sems, o_sems,
    st_s, st_r, gh_s, gh_r, l1s, l1r, l2s, l2r, sz_s, sz_r, ts, tr, ts2, tr2, ws, wr, ws2, wr2,
):
    me = lax.axis_index("vocab")
    z = lax.axis_index("dp")
    c = lax.rem(me, NC)
    chip = lax.div(me, NC)
    x = lax.rem(chip, NS)
    y = lax.div(chip, NS)
    a = x + c * (y - x)
    b = y + c * (x - y)

    def place(cc, bb, aa):
        yy = bb + cc * (aa - bb)
        xx = aa + cc * (bb - aa)
        return {"vocab": (yy * NS + xx) * NC + cc}

    sibling = {"vocab": chip * NC + 1 - c}

    def at_z(zz):
        return {"dp": zz}

    def owns3(zz):
        return lax.rem(zz, 3) == 0

    def tile_of(zz, s):
        return 16 + lax.div(zz, 3) if s == 2 else zz + 8 * s

    def rcopy(src, dst, ss, sr, dev):
        return pltpu.make_async_remote_copy(
            src_ref=src, dst_ref=dst, send_sem=ss, recv_sem=sr, device_id=dev, device_id_type=MESH
        )

    def got(ref, sem):
        rcopy(ref, ref, sem, sem, sibling).wait_recv()

    def sent(ref, sem):
        rcopy(ref, ref, sem, sem, sibling).wait_send()

    class Gather:
        def __init__(self, block, line, half, sems):
            self.block, self.line, self.half = block, line, half
            self.s, self.r = sems

        def first(self):
            for d in range(1, NS):
                ref = self.block(c, b, a)
                to = place(c, b, mod(a + d, NS))
                rcopy(ref, ref, self.s.at[d - 1], self.r.at[d - 1], to).start()

        def _side(self, bb, i):
            ref = self.line(c, bb)
            rcopy(ref, ref, self.s.at[7 + i], self.r.at[7 + i], sibling).start()

        def second(self):
            for d in range(1, NS):
                got(self.block(c, b, mod(a - d, NS)), self.r.at[d - 1])
            ref = self.line(c, b)
            for i, d in enumerate((1, -1)):
                rcopy(ref, ref, self.s.at[3 + i], self.r.at[3 + i], place(c, mod(b + d, NS), a)).start()
            self._side(b, 0)

        def relay(self):
            for i, d in enumerate((1, -1)):
                bb = mod(b - d, NS)
                got(self.line(c, bb), self.r.at[3 + i])
                ref = self.half(c, bb, i)
                rcopy(ref, ref, self.s.at[5 + i], self.r.at[5 + i], place(c, mod(b + d, NS), a)).start()
                self._side(bb, 1 + i)

        def last(self):
            bb = mod(b + 2, NS)
            for i in range(2):
                got(self.half(c, bb, i), self.r.at[5 + i])
            self._side(bb, 3)

        def finish(self):
            for i, d in enumerate((0, -1, 1, 2)):
                got(self.line(1 - c, mod(a + d, NS)), self.r.at[7 + i])

        def drain(self):
            for i in range(3):
                sent(self.block(c, b, a), self.s.at[i])
            for i in range(2):
                sent(self.line(c, b), self.s.at[3 + i])
                sent(self.half(c, b, i), self.s.at[5 + i])
            for i in range(4):
                sent(self.line(c, b), self.s.at[7 + i])

    own_h = Gather(
        lambda cc, bb, aa: hown.at[cc, bb, aa],
        lambda cc, bb: hown.at[cc, bb],
        lambda cc, bb, i: hown.at[cc, bb, pl.ds(2 * i, 2)],
        h_sems,
    )
    def probs_gather(part, sems):
        rows = pl.ds(part * HALF, HALF)
        return Gather(
            lambda cc, bb, aa: pbuf.at[cc, bb, aa, rows],
            lambda cc, bb: pbuf.at[cc, bb, :, rows],
            lambda cc, bb, i: pbuf.at[cc, bb, pl.ds(2 * i, 2), rows],
            sems,
        )

    probs = [probs_gather(0, p_sems), probs_gather(1, q_sems)]
    others = pl.ds(KEPT, ALL - KEPT)
    other_h = Gather(
        lambda cc, bb, aa: hall.at[cc, bb, aa, :, others],
        lambda cc, bb: hall.at[cc, bb, :, :, others],
        lambda cc, bb, i: hall.at[cc, bb, pl.ds(2 * i, 2), :, others],
        o_sems,
    )

    w_copy = pltpu.make_async_copy(w_hbm, w_ref, w_sem)
    w_copy.start()

    barrier = pltpu.get_barrier_semaphore()

    @pl.loop(1, NV)
    def _(d):
        pl.semaphore_signal(
            barrier, inc=1, device_id={"vocab": mod(me + d, NV)}, device_id_type=MESH
        )

    @pl.loop(1, NZ)
    def _(d):
        pl.semaphore_signal(barrier, inc=1, device_id=at_z(mod(z + d, NZ)), device_id_type=MESH)

    hown[c, b, a] = ht_ref[...]
    pbuf[c, b, a] = probs_ref[...]

    local = tiles_ref[...] - me * TILES
    local = jnp.where((local >= 0) & (local < TILES), local, 32)
    listed = lax.broadcasted_iota(jnp.int32, (NV, ROWS), 0) < count_ref[...]
    local = jnp.where(listed, local, -1).astype(F32).astype(BF16)
    slot = lax.shift_right_logical(lax.broadcasted_iota(jnp.int32, (NV, NV * RG), 1), 4)
    slot_b = lax.shift_right_logical(slot, 2) & 3
    slot_a = slot & 3
    position = jnp.where(slot < 16, slot_b * 8 + slot_a * 2, slot_a * 8 + slot_b * 2 + 1)
    spread = position == lax.broadcasted_iota(jnp.int32, (NV, NV * RG), 0)
    z_ref[...] = lax.dot_general(
        local, jnp.where(spread, 1.0, 0.0).astype(BF16), (((0,), (0,)), ((), ())),
        preferred_element_type=F32,
    )

    @pl.when(jnp.logical_not(owns3(z)))
    def _():
        t_in[2] = jnp.zeros((ALL, TILE), BF16)

    pl.semaphore_wait(barrier, NV - 1 + NZ - 1)

    for one in probs:
        one.first()
    own_h.first()
    for d in range(1, NZ):
        rcopy(
            hown.at[c, b, a], zin.at[NZ - d], zhs.at[d - 1], zhr.at[d - 1],
            at_z(mod(z + d, NZ)),
        ).start()
    for one in probs:
        one.second()
    own_h.second()
    for one in probs:
        one.relay()

    own = lax.rem(lax.broadcasted_iota(jnp.int32, (RG, NV * RG), 1), RG) == (
        lax.broadcasted_iota(jnp.int32, (RG, NV * RG), 0)
    )

    def place_rows(g):
        rows = pl.ds(pl.multiple_of(g * RG, RG), RG)
        spot = jnp.where(own, z_ref[rows, :], -1.0)
        blocks = [jnp.where(spot == float(n), 1.0, 0.0).astype(BF16) for n in range(TILES)]
        blocks.append(jnp.where(spot >= 0.0, 1.0, 0.0).astype(BF16))
        entries = pbuf[:, :, :, rows, :].reshape(NV * RG, TILE)
        placed = jnp.dot(jnp.concatenate(blocks, axis=0), entries, preferred_element_type=F32)
        for n in range(TILES):
            targ_ref[n, rows, :] = placed[n * RG : (n + 1) * RG].astype(BF16)
        mass_ref[rows, :] = placed[TILES * RG :]

    for part in range(2):
        probs[part].last()
        probs[part].finish()
        pl.loop(part * HALF // RG, (part + 1) * HALF // RG, unroll=2)(place_rows)
        rows = pl.ds(part * HALF, HALF)
        for d in range(1, NZ):
            to = mod(z + d, NZ)
            there = pl.ds((NZ - d) * ROWS + part * HALF, HALF)
            for s in range(2):
                rcopy(
                    targ_ref.at[tile_of(to, s), rows], t_in.at[s, there], ts, tr, at_z(to)
                ).start()

            @pl.when(owns3(to))
            def _():
                rcopy(
                    targ_ref.at[tile_of(to, 2), rows], t_in.at[2, there],
                    ts2.at[d], tr2, at_z(to),
                ).start()

        if part == 0:
            own_h.relay()
            for d in range(1, NZ):
                got(zin.at[NZ - d], zhr.at[d - 1])
            parts = [hown[c, b, a]] + [zin[d] for d in range(1, NZ)]
            hall[c, b, a] = jnp.concatenate(parts, axis=1)
            other_h.first()

    for s in range(2):
        t_in[s, 0:ROWS] = targ_ref[tile_of(z, s)]

    @pl.when(owns3(z))
    def _():
        t_in[2, 0:ROWS] = targ_ref[tile_of(z, 2)]

    own_h.last()
    own_h.finish()
    other_h.second()
    w_copy.wait()
    for i in range(NV // 2):
        yy, xx = i // NS, i % NS
        pair = jnp.concatenate([hown[0, yy, xx], hown[1, xx, yy]], axis=0)
        h_ref[:, i * 2 * BLK : (i + 1) * 2 * BLK] = pair.T

    peak = jnp.full((ROWS, TILE), -jnp.inf, F32)
    for lo, width in COLS:
        part = jnp.dot(h_ref[...], w_ref[:, lo : lo + width], preferred_element_type=F32)
        for t in range(width // TILE):
            one = part[:, t * TILE : (t + 1) * TILE]
            logit_ref[tile_rows(lo // TILE + t), :] = one
            peak = jnp.maximum(peak, one)
    peak = jnp.max(peak, axis=1, keepdims=True)
    mass = jnp.zeros((ROWS, TILE), F32)
    for t in range(TILES):
        mass = mass + jnp.exp(logit_ref[tile_rows(t), :] - peak)
    mass = jnp.sum(mass, axis=1, keepdims=True)

    lane = lax.broadcasted_iota(jnp.int32, (ROWS, TILE), 1)

    def message_of(first, second):
        packed = jnp.where(lane == 0, first, jnp.where(lane == 1, second, 0.0))
        packed = jnp.concatenate([packed, jnp.zeros((4 * TILE - ROWS, TILE), F32)], axis=0).T
        return jnp.concatenate(
            [packed[i : i + 1, k * TILE : (k + 1) * TILE] for i in range(2) for k in range(4)],
            axis=0,
        )

    message = message_of(peak, mass)
    stat_out[...] = message
    stat_in[me] = message

    @pl.loop(1, NV)
    def _(d):
        rcopy(stat_out, stat_in.at[me], st_s, st_r, {"vocab": mod(me + d, NV)}).start()

    for s in range(SLOTS):
        cols = tile_cols(tile_of(z, s))
        pieces = []
        for i in range(NV):
            cc, bb, aa = i // 16, i // 4 % 4, i % 4
            v = (bb * NS + aa) * NC if cc == 0 else (aa * NS + bb) * NC + 1
            pieces.append(w_ref[v * BLK : (v + 1) * BLK, cols])
        wt_ref[s * TILE : (s + 1) * TILE, :] = jnp.concatenate(pieces, axis=0).T

    teacher = jnp.sum(mass_ref[...], axis=1, keepdims=True)
    scale = 1.0 / teacher
    mass_ref[...] = jnp.broadcast_to(LOSS_SCALE * scale, (ROWS, TILE))
    scale_rows = message_of(LOSS_SCALE * scale, jnp.log(teacher))
    cross = jnp.zeros((ROWS, TILE), F32)
    for t in range(TILES):
        cross = cross + targ_ref[t].astype(F32) * logit_ref[tile_rows(t), :]
    entries = probs_ref[...].astype(F32)
    counts = jnp.broadcast_to(count_ref[...].astype(F32), (TILE, ROWS)).T
    weighted = jnp.where(counts > me.astype(F32), entries * jnp.log(entries), 0.0)
    shares = jnp.sum((weighted - cross) * scale)

    got(stat_in.at[pl.ds(0, NV - 1)], st_r)
    stats = stat_in[...]
    peaks, masses = stats[:, 0:4, :], stats[:, 4:8, :]
    top = jnp.max(peaks, axis=0)
    real = (
        lax.broadcasted_iota(jnp.int32, (4, TILE), 0) * TILE
        + lax.broadcasted_iota(jnp.int32, (4, TILE), 1)
    ) < ROWS
    total = jnp.where(real, jnp.sum(masses * jnp.exp(peaks - top[None]), axis=0), 1.0)
    log_norm = jnp.where(real, top + jnp.log(total), 0.0)
    stat_z[0] = jnp.concatenate([log_norm, scale_rows[0:4]], axis=0)
    for d in range(1, NZ):
        rcopy(stat_z.at[0], stat_z.at[NZ - d], sz_s, sz_r, at_z(mod(z + d, NZ))).start()
    ln_ref[...] = to_all_lanes(log_norm)
    common = jnp.sum(jnp.where(real, log_norm - scale_rows[4:8], 0.0)) * (1.0 / NV)
    l1[me] = jnp.broadcast_to(shares + common, (8, TILE))

    @pl.loop(1, NV)
    def _(d):
        rcopy(l1.at[me], l1.at[me], l1s, l1r, {"vocab": mod(me + d, NV)}).start()

    @pl.loop(0, TILES)
    def _(t):
        soft = LOSS_SCALE * jnp.exp(logit_ref[tile_rows(t), :] - ln_ref[...])
        g_ref[:, tile_cols(t)] = (soft - targ_ref[t].astype(F32) * mass_ref[...]).astype(BF16)

    @pl.loop(0, 4)
    def _(i):
        rows = pl.ds(pl.multiple_of(i * 512, 512), 512)
        part = lax.dot_general(
            w_ref[rows, :], g_ref[...], (((1,), (1,)), ((), ())), preferred_element_type=F32
        )
        ghs[pl.ds(i * 8, 8)] = part.astype(BF16).reshape(8, BLK, ROWS)

    ghr[me] = ghs[me]
    hall[:, :, :, :, 0:KEPT] = hown[:, :, :, :, 0:KEPT]

    other_h.relay()
    other_h.last()

    @pl.loop(1, NV)
    def _(d):
        to = mod(me + d, NV)
        rcopy(ghs.at[to], ghr.at[me], gh_s, gh_r, {"vocab": to}).start()

    got(l1.at[pl.ds(0, NV - 1)], l1r)
    l2[z] = jnp.sum(l1[...], axis=0)

    @pl.loop(1, NZ)
    def _(d):
        rcopy(l2.at[z], l2.at[z], l2s, l2r, at_z(mod(z + d, NZ))).start()

    got(stat_z.at[pl.ds(0, NZ - 1)], sz_r)
    lnf_ref[...] = jnp.concatenate(
        [flat_row(stat_z[d, 0:4])[:, :ROWS] for d in range(NZ)], axis=1
    )
    for d in range(NZ):
        col_ref[d * ROWS : (d + 1) * ROWS, :] = to_all_lanes(stat_z[d, 4:8])
    other_h.finish()

    @pl.loop(0, ALL // STEP)
    def _(k):
        lanes = pl.ds(pl.multiple_of(k * STEP, STEP), STEP)
        rows = hall[:, :, :, :, lanes].reshape(D, STEP)
        part = jnp.dot(wt_ref[...], rows, preferred_element_type=F32)
        soft = (LOSS_SCALE * jnp.exp(part - lnf_ref[:, lanes])).T
        for s in range(SLOTS):
            logit_ref[pl.ds(pl.multiple_of(s * ALL + k * STEP, STEP), STEP), :] = (
                soft[:, s * TILE : (s + 1) * TILE]
            )

    got(t_in.at[pl.ds(0, 2), pl.ds(ROWS, ALL - ROWS)], tr)

    @pl.when(owns3(z))
    def _():
        got(t_in.at[2, pl.ds(ROWS, ALL - ROWS)], tr2)

    @pl.loop(0, ALL // STEP)
    def _(k):
        rows = pl.ds(pl.multiple_of(k * STEP, STEP), STEP)
        for s in range(SLOTS):
            soft = logit_ref[pl.ds(pl.multiple_of(s * ALL + k * STEP, STEP), STEP), :]
            grad_ref[rows, s * TILE : (s + 1) * TILE] = (
                soft - t_in[s, rows, :].astype(F32) * col_ref[rows, :]
            ).astype(BF16)

    def head_block(j):
        yy, xx = lax.div(j, 2), 2 * lax.rem(j, 2)
        total = jnp.zeros((SLICE, WIDE), F32)
        for k in range(ALL // STEP):
            lanes = slice(k * STEP, (k + 1) * STEP)
            part = [
                hall[0, yy, xx, :, lanes], hall[1, xx, yy, :, lanes],
                hall[0, yy, xx + 1, :, lanes], hall[1, xx + 1, yy, :, lanes],
            ]
            total = total + jnp.dot(
                jnp.concatenate(part, axis=0), grad_ref[lanes, :], preferred_element_type=F32
            )
        return total.astype(BF16)

    @pl.loop(1, NZ)
    def _(i):
        j = mod(z + i, NZ)
        done = head_block(j)
        for s in range(SLOTS):
            gws[i, s] = done[:, s * TILE : (s + 1) * TILE]
        for s in range(2):
            rcopy(gws.at[i, s], gw_ref.at[:, tile_cols(tile_of(z, s))], ws, wr, at_z(j)).start()

        @pl.when(owns3(z))
        def _():
            rcopy(
                gws.at[i, 2], gw_ref.at[:, tile_cols(tile_of(z, 2))],
                ws2, wr2.at[lax.div(z, 3)], at_z(j),
            ).start()

    done = head_block(z)
    for s in range(2):
        gw_ref[:, tile_cols(tile_of(z, s))] = done[:, s * TILE : (s + 1) * TILE]

    @pl.when(owns3(z))
    def _():
        gw_ref[:, tile_cols(tile_of(z, 2))] = done[:, 2 * TILE :]

    got(ghr.at[pl.ds(0, NV - 1)], gh_r)
    sum_h = jnp.zeros((BLK, ROWS), F32)
    for i in range(NV):
        sum_h = sum_h + ghr[i].astype(F32)
    gh_ref[...] = sum_h.astype(BF16)
    got(l2.at[pl.ds(0, NZ - 1)], l2r)
    loss_ref[...] = jnp.sum(l2[...], axis=0) * (1.0 / (ROWS * NZ))

    for one in probs:
        one.drain()
    own_h.drain()
    other_h.drain()
    for d in range(1, NZ):
        sent(hown.at[c, b, a], zhs.at[d - 1])
    sent(stat_in.at[pl.ds(0, NV - 1)], st_s)
    sent(ghr.at[pl.ds(0, NV - 1)], gh_s)
    sent(l1.at[pl.ds(0, NV - 1)], l1s)
    sent(l2.at[pl.ds(0, NZ - 1)], l2s)
    sent(stat_z.at[pl.ds(0, NZ - 1)], sz_s)
    sent(t_in.at[pl.ds(0, 2), pl.ds(ROWS, ALL - ROWS)], ts)
    for d in range(1, NZ):

        @pl.when(owns3(mod(z + d, NZ)))
        def _():
            sent(targ_ref.at[0], ts2.at[d])

    sent(gws.at[pl.ds(1, NZ - 1), pl.ds(0, 2)], ws)

    @pl.when(owns3(z))
    def _():
        sent(gws.at[pl.ds(1, NZ - 1), 2], ws2)

    got(gws.at[pl.ds(1, NZ - 1), pl.ds(0, 2)], wr)
    for i in range(SLOTS):

        @pl.when(z != 3 * i)
        def _():
            got(gws.at[0, 0], wr2.at[i])


def shards(hidden, head_weight, kept_tiles, kept_count, teacher_probs):
    vmem = pl.BlockSpec(memory_space=pltpu.VMEM)
    dma = pltpu.SemaphoreType.DMA
    loss, gh, gw = pl.pallas_call(
        kernel,
        out_shape=(
            jax.ShapeDtypeStruct((8, TILE), F32),
            jax.ShapeDtypeStruct((BLK, ROWS), BF16),
            jax.ShapeDtypeStruct((SLICE, VOC), BF16),
        ),
        in_specs=[vmem, pl.BlockSpec(memory_space=pl.ANY), vmem, vmem, vmem],
        out_specs=(vmem, vmem, vmem),
        scratch_shapes=[
            pltpu.VMEM((D, VOC), BF16),
            pltpu.VMEM((NC, NS, NS, BLK, ALL), BF16),
            pltpu.VMEM((NC, NS, NS, BLK, ROWS), BF16),
            pltpu.VMEM((NZ, BLK, ROWS), BF16),
            pltpu.VMEM((1, ALL), F32),
            pltpu.VMEM((ALL, TILE), F32),
            pltpu.VMEM((ROWS, D), BF16),
            pltpu.VMEM((NC, NS, NS, ROWS, TILE), BF16),
            pltpu.VMEM((SLOTS * ALL, TILE), F32),
            pltpu.VMEM((TILES, ROWS, TILE), BF16),
            pltpu.VMEM((ROWS, VOC), BF16),
            pltpu.VMEM((ROWS, NV * RG), F32),
            pltpu.VMEM((ROWS, TILE), F32),
            pltpu.VMEM((ROWS, TILE), F32),
            pltpu.VMEM((WIDE, D), BF16),
            pltpu.VMEM((SLOTS, ALL, TILE), BF16),
            pltpu.VMEM((ALL, WIDE), BF16),
            pltpu.VMEM((NZ, SLOTS, SLICE, TILE), BF16),
            pltpu.VMEM((8, TILE), F32),
            pltpu.VMEM((NV, 8, TILE), F32),
            pltpu.VMEM((NZ, 8, TILE), F32),
            pltpu.VMEM((NV, BLK, ROWS), BF16),
            pltpu.VMEM((NV, BLK, ROWS), BF16),
            pltpu.VMEM((NV, 8, TILE), F32),
            pltpu.VMEM((NZ, 8, TILE), F32),
            dma, dma((NZ - 1,)), dma((NZ - 1,)),
            [dma((11,)), dma((11,))], [dma((11,)), dma((11,))], [dma((11,)), dma((11,))], [dma((11,)), dma((11,))],
            dma, dma, dma, dma, dma, dma, dma, dma, dma, dma,
            dma, dma, dma((NZ,)), dma, dma, dma, dma, dma((SLOTS,)),
        ],
        compiler_params=pltpu.CompilerParams(
            collective_id=0, has_side_effects=True, vmem_limit_bytes=60 * 1024 * 1024
        ),
        cost_estimate=pl.CostEstimate(
            flops=8 * ROWS * D * VOC, bytes_accessed=2 * D * VOC, transcendentals=3 * ROWS * VOC
        ),
    )(
        hidden.T,
        head_weight,
        kept_tiles.T,
        kept_count.reshape(1, ROWS),
        teacher_probs.reshape(ROWS, TILE),
    )
    return loss[0, 0], gh.T, gw


def solution(mesh):
    return jax.shard_map(
        shards,
        mesh=mesh,
        in_specs=(
            P("dp", "vocab"),
            P(None, "vocab"),
            P("dp", None),
            P("dp"),
            P("dp", "vocab", None),
        ),
        out_specs=(P(), P("dp", "vocab"), P("dp", "vocab")),
        check_vma=False,
    )
```

```python
import jax
import jax.numpy as jnp
from jax import lax
from jax.experimental import pallas as pl
from jax.experimental.pallas import tpu as pltpu
from jax.sharding import PartitionSpec as P

LOSS_SCALE = 1024.0
MESH = pl.DeviceIdType.MESH
NS = 4
NC = 2
NV = NS * NS * NC
NZ = 8
ROWS = 448
D = 2048
BLK = D // NV
TILE = 128
VOC = 2432
TILES = VOC // TILE
SLOTS = 3
WIDE = SLOTS * TILE
SLICE = D // NZ
RG = 16
PARTS = ((0, 96), (96, 160), (256, 192))
ALL = ROWS * NZ
KEPT = 3 * TILE
STEP = 512
COLS = ((0, 512), (512, 512), (1024, 512), (1536, 512), (2048, 384))
F32 = jnp.float32
BF16 = jnp.bfloat16


def mod(a, n):
    return lax.rem(a + n, n)


def flat_row(rows4):
    return jnp.concatenate([rows4[a : a + 1, :] for a in range(4)], axis=1)


def to_all_lanes(rows4):
    return jnp.broadcast_to(flat_row(rows4), (TILE, 4 * TILE)).T[:ROWS, :]


def tile_cols(t):
    return pl.ds(pl.multiple_of(t * TILE, TILE), TILE)


def tile_rows(t):
    return slice(t * ROWS, (t + 1) * ROWS) if isinstance(t, int) else pl.ds(
        pl.multiple_of(t * ROWS, ROWS), ROWS
    )


def kernel(
    ht_ref, w_hbm, tiles_ref, count_ref, probs_ref,
    loss_ref, gh_ref, gw_ref,
    w_ref, hall, hown, zin, lnf_ref, col_ref, h_ref, pbuf, logit_ref, targ_ref, g_ref, z_ref, mass_ref, ln_ref,
    wt_ref, t_in, grad_ref, gws, stat_out, stat_in, stat_z, ghs, ghr, l1, l2,
    w_sem, zhs, zhr, h_sems, p_sems, q_sems, v_sems, o_sems,
    st_s, st_r, gh_s, gh_r, l1s, l1r, l2s, l2r, sz_s, sz_r, ts, tr, ts2, tr2, ws, wr, ws2, wr2,
):
    me = lax.axis_index("vocab")
    z = lax.axis_index("dp")
    c = lax.rem(me, NC)
    chip = lax.div(me, NC)
    x = lax.rem(chip, NS)
    y = lax.div(chip, NS)
    a = x + c * (y - x)
    b = y + c * (x - y)

    def place(cc, bb, aa):
        yy = bb + cc * (aa - bb)
        xx = aa + cc * (bb - aa)
        return {"vocab": (yy * NS + xx) * NC + cc}

    sibling = {"vocab": chip * NC + 1 - c}

    def at_z(zz):
        return {"dp": zz}

    def owns3(zz):
        return lax.rem(zz, 3) == 0

    def tile_of(zz, s):
        return 16 + lax.div(zz, 3) if s == 2 else zz + 8 * s

    def rcopy(src, dst, ss, sr, dev):
        return pltpu.make_async_remote_copy(
            src_ref=src, dst_ref=dst, send_sem=ss, recv_sem=sr, device_id=dev, device_id_type=MESH
        )

    def got(ref, sem):
        rcopy(ref, ref, sem, sem, sibling).wait_recv()

    def sent(ref, sem):
        rcopy(ref, ref, sem, sem, sibling).wait_send()

    class Gather:
        def __init__(self, block, line, half, sems):
            self.block, self.line, self.half = block, line, half
            self.s, self.r = sems

        def first(self):
            for d in range(1, NS):
                ref = self.block(c, b, a)
                to = place(c, b, mod(a + d, NS))
                rcopy(ref, ref, self.s.at[d - 1], self.r.at[d - 1], to).start()

        def _side(self, bb, i):
            ref = self.line(c, bb)
            rcopy(ref, ref, self.s.at[7 + i], self.r.at[7 + i], sibling).start()

        def second(self):
            for d in range(1, NS):
                got(self.block(c, b, mod(a - d, NS)), self.r.at[d - 1])
            ref = self.line(c, b)
            for i, d in enumerate((1, -1)):
                rcopy(ref, ref, self.s.at[3 + i], self.r.at[3 + i], place(c, mod(b + d, NS), a)).start()
            self._side(b, 0)

        def relay(self):
            for i, d in enumerate((1, -1)):
                bb = mod(b - d, NS)
                got(self.line(c, bb), self.r.at[3 + i])
                ref = self.half(c, bb, i)
                rcopy(ref, ref, self.s.at[5 + i], self.r.at[5 + i], place(c, mod(b + d, NS), a)).start()
                self._side(bb, 1 + i)

        def last(self):
            bb = mod(b + 2, NS)
            for i in range(2):
                got(self.half(c, bb, i), self.r.at[5 + i])
            self._side(bb, 3)

        def finish(self):
            for i, d in enumerate((0, -1, 1, 2)):
                got(self.line(1 - c, mod(a + d, NS)), self.r.at[7 + i])

        def drain(self):
            for i in range(3):
                sent(self.block(c, b, a), self.s.at[i])
            for i in range(2):
                sent(self.line(c, b), self.s.at[3 + i])
                sent(self.half(c, b, i), self.s.at[5 + i])
            for i in range(4):
                sent(self.line(c, b), self.s.at[7 + i])

    own_h = Gather(
        lambda cc, bb, aa: hown.at[cc, bb, aa],
        lambda cc, bb: hown.at[cc, bb],
        lambda cc, bb, i: hown.at[cc, bb, pl.ds(2 * i, 2)],
        h_sems,
    )
    def probs_gather(part, sems):
        rows = pl.ds(*PARTS[part])
        return Gather(
            lambda cc, bb, aa: pbuf.at[cc, bb, aa, rows],
            lambda cc, bb: pbuf.at[cc, bb, :, rows],
            lambda cc, bb, i: pbuf.at[cc, bb, pl.ds(2 * i, 2), rows],
            sems,
        )

    probs = [probs_gather(i, sems) for i, sems in enumerate((p_sems, q_sems, v_sems))]
    others = pl.ds(KEPT, ALL - KEPT)
    other_h = Gather(
        lambda cc, bb, aa: hall.at[cc, bb, aa, :, others],
        lambda cc, bb: hall.at[cc, bb, :, :, others],
        lambda cc, bb, i: hall.at[cc, bb, pl.ds(2 * i, 2), :, others],
        o_sems,
    )

    w_copy = pltpu.make_async_copy(w_hbm, w_ref, w_sem)
    w_copy.start()

    barrier = pltpu.get_barrier_semaphore()

    @pl.loop(1, NV)
    def _(d):
        pl.semaphore_signal(
            barrier, inc=1, device_id={"vocab": mod(me + d, NV)}, device_id_type=MESH
        )

    @pl.loop(1, NZ)
    def _(d):
        pl.semaphore_signal(barrier, inc=1, device_id=at_z(mod(z + d, NZ)), device_id_type=MESH)

    hown[c, b, a] = ht_ref[...]
    pbuf[c, b, a] = probs_ref[...]

    local = tiles_ref[...] - me * TILES
    local = jnp.where((local >= 0) & (local < TILES), local, 32)
    listed = lax.broadcasted_iota(jnp.int32, (NV, ROWS), 0) < count_ref[...]
    local = jnp.where(listed, local, -1).astype(F32).astype(BF16)
    slot = lax.shift_right_logical(lax.broadcasted_iota(jnp.int32, (NV, NV * RG), 1), 4)
    slot_b = lax.shift_right_logical(slot, 2) & 3
    slot_a = slot & 3
    position = jnp.where(slot < 16, slot_b * 8 + slot_a * 2, slot_a * 8 + slot_b * 2 + 1)
    spread = position == lax.broadcasted_iota(jnp.int32, (NV, NV * RG), 0)
    z_ref[...] = lax.dot_general(
        local, jnp.where(spread, 1.0, 0.0).astype(BF16), (((0,), (0,)), ((), ())),
        preferred_element_type=F32,
    )

    @pl.when(jnp.logical_not(owns3(z)))
    def _():
        t_in[2] = jnp.zeros((ALL, TILE), BF16)

    pl.semaphore_wait(barrier, NV - 1 + NZ - 1)

    for one in probs:
        one.first()
    own_h.first()
    for d in range(1, NZ):
        rcopy(
            hown.at[c, b, a], zin.at[NZ - d], zhs.at[d - 1], zhr.at[d - 1],
            at_z(mod(z + d, NZ)),
        ).start()
    for one in probs:
        one.second()
    own_h.second()
    for one in probs[:2]:
        one.relay()
    for d in range(1, NZ):
        got(zin.at[NZ - d], zhr.at[d - 1])
    hall[c, b, a] = jnp.concatenate([hown[c, b, a]] + [zin[d] for d in range(1, NZ)], axis=1)
    other_h.first()

    own = lax.rem(lax.broadcasted_iota(jnp.int32, (RG, NV * RG), 1), RG) == (
        lax.broadcasted_iota(jnp.int32, (RG, NV * RG), 0)
    )

    def place_rows(g):
        rows = pl.ds(pl.multiple_of(g * RG, RG), RG)
        spot = jnp.where(own, z_ref[rows, :], -1.0)
        blocks = [jnp.where(spot == float(n), 1.0, 0.0).astype(BF16) for n in range(TILES)]
        blocks.append(jnp.where(spot >= 0.0, 1.0, 0.0).astype(BF16))
        entries = pbuf[:, :, :, rows, :].reshape(NV * RG, TILE)
        placed = jnp.dot(jnp.concatenate(blocks, axis=0), entries, preferred_element_type=F32)
        for n in range(TILES):
            targ_ref[n, rows, :] = placed[n * RG : (n + 1) * RG].astype(BF16)
        mass_ref[rows, :] = placed[TILES * RG :]

    for part, (low, size) in enumerate(PARTS):
        probs[part].last()
        probs[part].finish()
        pl.loop(low // RG, (low + size) // RG, unroll=2)(place_rows)
        rows = pl.ds(low, size)
        for d in range(1, NZ):
            to = mod(z + d, NZ)
            there = pl.ds((NZ - d) * ROWS + low, size)
            for s in range(2):
                rcopy(
                    targ_ref.at[tile_of(to, s), rows], t_in.at[s, there], ts, tr, at_z(to)
                ).start()

            @pl.when(owns3(to))
            def _():
                rcopy(
                    targ_ref.at[tile_of(to, 2), rows], t_in.at[2, there],
                    ts2.at[d], tr2, at_z(to),
                ).start()

        if part == 0:
            probs[2].relay()
            own_h.relay()
        if part == 1:
            other_h.second()

    for s in range(2):
        t_in[s, 0:ROWS] = targ_ref[tile_of(z, s)]

    @pl.when(owns3(z))
    def _():
        t_in[2, 0:ROWS] = targ_ref[tile_of(z, 2)]

    own_h.last()
    own_h.finish()
    w_copy.wait()
    for i in range(NV // 2):
        yy, xx = i // NS, i % NS
        pair = jnp.concatenate([hown[0, yy, xx], hown[1, xx, yy]], axis=0)
        h_ref[:, i * 2 * BLK : (i + 1) * 2 * BLK] = pair.T

    peak = jnp.full((ROWS, TILE), -jnp.inf, F32)
    for lo, width in COLS:
        part = jnp.dot(h_ref[...], w_ref[:, lo : lo + width], preferred_element_type=F32)
        for t in range(width // TILE):
            one = part[:, t * TILE : (t + 1) * TILE]
            logit_ref[tile_rows(lo // TILE + t), :] = one
            peak = jnp.maximum(peak, one)
    peak = jnp.max(peak, axis=1, keepdims=True)
    mass = jnp.zeros((ROWS, TILE), F32)
    for t in range(TILES):
        mass = mass + jnp.exp(logit_ref[tile_rows(t), :] - peak)
    mass = jnp.sum(mass, axis=1, keepdims=True)

    lane = lax.broadcasted_iota(jnp.int32, (ROWS, TILE), 1)

    def message_of(first, second):
        packed = jnp.where(lane == 0, first, jnp.where(lane == 1, second, 0.0))
        packed = jnp.concatenate([packed, jnp.zeros((4 * TILE - ROWS, TILE), F32)], axis=0).T
        return jnp.concatenate(
            [packed[i : i + 1, k * TILE : (k + 1) * TILE] for i in range(2) for k in range(4)],
            axis=0,
        )

    message = message_of(peak, mass)
    stat_out[...] = message
    stat_in[me] = message

    @pl.loop(1, NV)
    def _(d):
        rcopy(stat_out, stat_in.at[me], st_s, st_r, {"vocab": mod(me + d, NV)}).start()

    for s in range(SLOTS):
        cols = tile_cols(tile_of(z, s))
        pieces = []
        for i in range(NV):
            cc, bb, aa = i // 16, i // 4 % 4, i % 4
            v = (bb * NS + aa) * NC if cc == 0 else (aa * NS + bb) * NC + 1
            pieces.append(w_ref[v * BLK : (v + 1) * BLK, cols])
        wt_ref[s * TILE : (s + 1) * TILE, :] = jnp.concatenate(pieces, axis=0).T

    teacher = jnp.sum(mass_ref[...], axis=1, keepdims=True)
    scale = 1.0 / teacher
    mass_ref[...] = jnp.broadcast_to(LOSS_SCALE * scale, (ROWS, TILE))
    scale_rows = message_of(LOSS_SCALE * scale, jnp.log(teacher))
    cross = jnp.zeros((ROWS, TILE), F32)
    for t in range(TILES):
        cross = cross + targ_ref[t].astype(F32) * logit_ref[tile_rows(t), :]
    entries = probs_ref[...].astype(F32)
    counts = jnp.broadcast_to(count_ref[...].astype(F32), (TILE, ROWS)).T
    weighted = jnp.where(counts > me.astype(F32), entries * jnp.log(entries), 0.0)
    shares = jnp.sum((weighted - cross) * scale)

    other_h.relay()

    got(stat_in.at[pl.ds(0, NV - 1)], st_r)
    stats = stat_in[...]
    peaks, masses = stats[:, 0:4, :], stats[:, 4:8, :]
    top = jnp.max(peaks, axis=0)
    real = (
        lax.broadcasted_iota(jnp.int32, (4, TILE), 0) * TILE
        + lax.broadcasted_iota(jnp.int32, (4, TILE), 1)
    ) < ROWS
    total = jnp.where(real, jnp.sum(masses * jnp.exp(peaks - top[None]), axis=0), 1.0)
    log_norm = jnp.where(real, top + jnp.log(total), 0.0)
    stat_z[0] = jnp.concatenate([log_norm, scale_rows[0:4]], axis=0)
    for d in range(1, NZ):
        rcopy(stat_z.at[0], stat_z.at[NZ - d], sz_s, sz_r, at_z(mod(z + d, NZ))).start()
    ln_ref[...] = to_all_lanes(log_norm)
    common = jnp.sum(jnp.where(real, log_norm - scale_rows[4:8], 0.0)) * (1.0 / NV)
    l1[me] = jnp.broadcast_to(shares + common, (8, TILE))

    @pl.loop(1, NV)
    def _(d):
        rcopy(l1.at[me], l1.at[me], l1s, l1r, {"vocab": mod(me + d, NV)}).start()

    @pl.loop(0, TILES)
    def _(t):
        soft = LOSS_SCALE * jnp.exp(logit_ref[tile_rows(t), :] - ln_ref[...])
        g_ref[:, tile_cols(t)] = (soft - targ_ref[t].astype(F32) * mass_ref[...]).astype(BF16)

    @pl.loop(0, 4)
    def _(i):
        rows = pl.ds(pl.multiple_of(i * 512, 512), 512)
        part = lax.dot_general(
            w_ref[rows, :], g_ref[...], (((1,), (1,)), ((), ())), preferred_element_type=F32
        )
        ghs[pl.ds(i * 8, 8)] = part.astype(BF16).reshape(8, BLK, ROWS)

    ghr[me] = ghs[me]
    hall[:, :, :, :, 0:KEPT] = hown[:, :, :, :, 0:KEPT]

    other_h.last()

    @pl.loop(1, NV)
    def _(d):
        to = mod(me + d, NV)
        rcopy(ghs.at[to], ghr.at[me], gh_s, gh_r, {"vocab": to}).start()

    got(l1.at[pl.ds(0, NV - 1)], l1r)
    l2[z] = jnp.sum(l1[...], axis=0)

    @pl.loop(1, NZ)
    def _(d):
        rcopy(l2.at[z], l2.at[z], l2s, l2r, at_z(mod(z + d, NZ))).start()

    got(stat_z.at[pl.ds(0, NZ - 1)], sz_r)
    lnf_ref[...] = jnp.concatenate(
        [flat_row(stat_z[d, 0:4])[:, :ROWS] for d in range(NZ)], axis=1
    )
    for d in range(NZ):
        col_ref[d * ROWS : (d + 1) * ROWS, :] = to_all_lanes(stat_z[d, 4:8])
    other_h.finish()

    @pl.loop(0, ALL // STEP)
    def _(k):
        lanes = pl.ds(pl.multiple_of(k * STEP, STEP), STEP)
        rows = hall[:, :, :, :, lanes].reshape(D, STEP)
        part = jnp.dot(wt_ref[...], rows, preferred_element_type=F32)
        soft = (LOSS_SCALE * jnp.exp(part - lnf_ref[:, lanes])).T
        for s in range(SLOTS):
            logit_ref[pl.ds(pl.multiple_of(s * ALL + k * STEP, STEP), STEP), :] = (
                soft[:, s * TILE : (s + 1) * TILE]
            )

    got(t_in.at[pl.ds(0, 2), pl.ds(ROWS, ALL - ROWS)], tr)

    @pl.when(owns3(z))
    def _():
        got(t_in.at[2, pl.ds(ROWS, ALL - ROWS)], tr2)

    @pl.loop(0, ALL // STEP)
    def _(k):
        rows = pl.ds(pl.multiple_of(k * STEP, STEP), STEP)
        for s in range(SLOTS):
            soft = logit_ref[pl.ds(pl.multiple_of(s * ALL + k * STEP, STEP), STEP), :]
            grad_ref[rows, s * TILE : (s + 1) * TILE] = (
                soft - t_in[s, rows, :].astype(F32) * col_ref[rows, :]
            ).astype(BF16)

    def head_block(j):
        yy, xx = lax.div(j, 2), 2 * lax.rem(j, 2)
        total = jnp.zeros((SLICE, WIDE), F32)
        for k in range(ALL // STEP):
            lanes = slice(k * STEP, (k + 1) * STEP)
            part = [
                hall[0, yy, xx, :, lanes], hall[1, xx, yy, :, lanes],
                hall[0, yy, xx + 1, :, lanes], hall[1, xx + 1, yy, :, lanes],
            ]
            total = total + jnp.dot(
                jnp.concatenate(part, axis=0), grad_ref[lanes, :], preferred_element_type=F32
            )
        return total.astype(BF16)

    @pl.loop(1, NZ)
    def _(i):
        j = mod(z + i, NZ)
        done = head_block(j)
        for s in range(SLOTS):
            gws[i, s] = done[:, s * TILE : (s + 1) * TILE]
        for s in range(2):
            rcopy(gws.at[i, s], gw_ref.at[:, tile_cols(tile_of(z, s))], ws, wr, at_z(j)).start()

        @pl.when(owns3(z))
        def _():
            rcopy(
                gws.at[i, 2], gw_ref.at[:, tile_cols(tile_of(z, 2))],
                ws2, wr2.at[lax.div(z, 3)], at_z(j),
            ).start()

    done = head_block(z)
    for s in range(2):
        gw_ref[:, tile_cols(tile_of(z, s))] = done[:, s * TILE : (s + 1) * TILE]

    @pl.when(owns3(z))
    def _():
        gw_ref[:, tile_cols(tile_of(z, 2))] = done[:, 2 * TILE :]

    got(ghr.at[pl.ds(0, NV - 1)], gh_r)
    sum_h = jnp.zeros((BLK, ROWS), F32)
    for i in range(NV):
        sum_h = sum_h + ghr[i].astype(F32)
    gh_ref[...] = sum_h.astype(BF16)
    got(l2.at[pl.ds(0, NZ - 1)], l2r)
    loss_ref[...] = jnp.sum(l2[...], axis=0) * (1.0 / (ROWS * NZ))

    for one in probs:
        one.drain()
    own_h.drain()
    other_h.drain()
    for d in range(1, NZ):
        sent(hown.at[c, b, a], zhs.at[d - 1])
    sent(stat_in.at[pl.ds(0, NV - 1)], st_s)
    sent(ghr.at[pl.ds(0, NV - 1)], gh_s)
    sent(l1.at[pl.ds(0, NV - 1)], l1s)
    sent(l2.at[pl.ds(0, NZ - 1)], l2s)
    sent(stat_z.at[pl.ds(0, NZ - 1)], sz_s)
    sent(t_in.at[pl.ds(0, 2), pl.ds(ROWS, ALL - ROWS)], ts)
    for d in range(1, NZ):

        @pl.when(owns3(mod(z + d, NZ)))
        def _():
            sent(targ_ref.at[0], ts2.at[d])

    sent(gws.at[pl.ds(1, NZ - 1), pl.ds(0, 2)], ws)

    @pl.when(owns3(z))
    def _():
        sent(gws.at[pl.ds(1, NZ - 1), 2], ws2)

    got(gws.at[pl.ds(1, NZ - 1), pl.ds(0, 2)], wr)
    for i in range(SLOTS):

        @pl.when(z != 3 * i)
        def _():
            got(gws.at[0, 0], wr2.at[i])


def shards(hidden, head_weight, kept_tiles, kept_count, teacher_probs):
    vmem = pl.BlockSpec(memory_space=pltpu.VMEM)
    dma = pltpu.SemaphoreType.DMA
    loss, gh, gw = pl.pallas_call(
        kernel,
        out_shape=(
            jax.ShapeDtypeStruct((8, TILE), F32),
            jax.ShapeDtypeStruct((BLK, ROWS), BF16),
            jax.ShapeDtypeStruct((SLICE, VOC), BF16),
        ),
        in_specs=[vmem, pl.BlockSpec(memory_space=pl.ANY), vmem, vmem, vmem],
        out_specs=(vmem, vmem, vmem),
        scratch_shapes=[
            pltpu.VMEM((D, VOC), BF16),
            pltpu.VMEM((NC, NS, NS, BLK, ALL), BF16),
            pltpu.VMEM((NC, NS, NS, BLK, ROWS), BF16),
            pltpu.VMEM((NZ, BLK, ROWS), BF16),
            pltpu.VMEM((1, ALL), F32),
            pltpu.VMEM((ALL, TILE), F32),
            pltpu.VMEM((ROWS, D), BF16),
            pltpu.VMEM((NC, NS, NS, ROWS, TILE), BF16),
            pltpu.VMEM((SLOTS * ALL, TILE), F32),
            pltpu.VMEM((TILES, ROWS, TILE), BF16),
            pltpu.VMEM((ROWS, VOC), BF16),
            pltpu.VMEM((ROWS, NV * RG), F32),
            pltpu.VMEM((ROWS, TILE), F32),
            pltpu.VMEM((ROWS, TILE), F32),
            pltpu.VMEM((WIDE, D), BF16),
            pltpu.VMEM((SLOTS, ALL, TILE), BF16),
            pltpu.VMEM((ALL, WIDE), BF16),
            pltpu.VMEM((NZ, SLOTS, SLICE, TILE), BF16),
            pltpu.VMEM((8, TILE), F32),
            pltpu.VMEM((NV, 8, TILE), F32),
            pltpu.VMEM((NZ, 8, TILE), F32),
            pltpu.VMEM((NV, BLK, ROWS), BF16),
            pltpu.VMEM((NV, BLK, ROWS), BF16),
            pltpu.VMEM((NV, 8, TILE), F32),
            pltpu.VMEM((NZ, 8, TILE), F32),
            dma, dma((NZ - 1,)), dma((NZ - 1,)),
            [dma((11,)), dma((11,))], [dma((11,)), dma((11,))], [dma((11,)), dma((11,))], [dma((11,)), dma((11,))], [dma((11,)), dma((11,))],
            dma, dma, dma, dma, dma, dma, dma, dma, dma, dma,
            dma, dma, dma((NZ,)), dma, dma, dma, dma, dma((SLOTS,)),
        ],
        compiler_params=pltpu.CompilerParams(
            collective_id=0, has_side_effects=True, vmem_limit_bytes=60 * 1024 * 1024
        ),
        cost_estimate=pl.CostEstimate(
            flops=8 * ROWS * D * VOC, bytes_accessed=2 * D * VOC, transcendentals=3 * ROWS * VOC
        ),
    )(
        hidden.T,
        head_weight,
        kept_tiles.T,
        kept_count.reshape(1, ROWS),
        teacher_probs.reshape(ROWS, TILE),
    )
    return loss[0, 0], gh.T, gw


def solution(mesh):
    return jax.shard_map(
        shards,
        mesh=mesh,
        in_specs=(
            P("dp", "vocab"),
            P(None, "vocab"),
            P("dp", None),
            P("dp"),
            P("dp", "vocab", None),
        ),
        out_specs=(P(), P("dp", "vocab"), P("dp", "vocab")),
        check_vma=False,
    )
```

```python
import jax
import jax.numpy as jnp
from jax import lax
from jax.experimental import pallas as pl
from jax.experimental.pallas import tpu as pltpu
from jax.sharding import PartitionSpec as P

LOSS_SCALE = 1024.0
MESH = pl.DeviceIdType.MESH
NS = 4
NC = 2
NV = NS * NS * NC
NZ = 8
ROWS = 448
D = 2048
BLK = D // NV
TILE = 128
VOC = 2432
TILES = VOC // TILE
SLOTS = 3
WIDE = SLOTS * TILE
SLICE = D // NZ
RG = 16
PARTS = ((0, 96), (96, 160), (256, 192))
ALL = ROWS * NZ
KEPT = 3 * TILE
STEP = 512
COLS = ((0, 512), (512, 512), (1024, 512), (1536, 512), (2048, 384))
F32 = jnp.float32
BF16 = jnp.bfloat16


def mod(a, n):
    return lax.rem(a + n, n)


def flat_row(rows4):
    return jnp.concatenate([rows4[a : a + 1, :] for a in range(4)], axis=1)


def to_all_lanes(rows4):
    return jnp.broadcast_to(flat_row(rows4), (TILE, 4 * TILE)).T[:ROWS, :]


def tile_cols(t):
    return pl.ds(pl.multiple_of(t * TILE, TILE), TILE)


def tile_rows(t):
    return slice(t * ROWS, (t + 1) * ROWS) if isinstance(t, int) else pl.ds(
        pl.multiple_of(t * ROWS, ROWS), ROWS
    )


def kernel(
    ht_ref, w_hbm, tiles_ref, count_ref, probs_ref,
    loss_ref, gh_ref, gw_ref,
    w_ref, hall, hown, zin, lnf_ref, col_ref, h_ref, pbuf, logit_ref, targ_ref, g_ref, z_ref, mass_ref, ln_ref,
    wt_ref, t_in, grad_ref, gws, stat_out, stat_in, stat_z, ghs, ghr, l1, l2,
    w_sem, zhs, zhr, h_sems, p_sems, q_sems, v_sems, o_sems,
    st_s, st_r, gh_s, gh_r, l1s, l1r, l2s, l2r, sz_s, sz_r, ts, tr, ts2, tr2, ws, wr, ws2, wr2,
):
    me = lax.axis_index("vocab")
    z = lax.axis_index("dp")
    c = lax.rem(me, NC)
    chip = lax.div(me, NC)
    x = lax.rem(chip, NS)
    y = lax.div(chip, NS)
    a = x + c * (y - x)
    b = y + c * (x - y)

    def place(cc, bb, aa):
        yy = bb + cc * (aa - bb)
        xx = aa + cc * (bb - aa)
        return {"vocab": (yy * NS + xx) * NC + cc}

    sibling = {"vocab": chip * NC + 1 - c}

    def at_z(zz):
        return {"dp": zz}

    def owns3(zz):
        return lax.rem(zz, 3) == 0

    def tile_of(zz, s):
        return 16 + lax.div(zz, 3) if s == 2 else zz + 8 * s

    def rcopy(src, dst, ss, sr, dev):
        return pltpu.make_async_remote_copy(
            src_ref=src, dst_ref=dst, send_sem=ss, recv_sem=sr, device_id=dev, device_id_type=MESH
        )

    def got(ref, sem):
        rcopy(ref, ref, sem, sem, sibling).wait_recv()

    def sent(ref, sem):
        rcopy(ref, ref, sem, sem, sibling).wait_send()

    class Gather:
        def __init__(self, block, line, half, sems):
            self.block, self.line, self.half = block, line, half
            self.s, self.r = sems

        def first(self):
            for d in range(1, NS):
                ref = self.block(c, b, a)
                to = place(c, b, mod(a + d, NS))
                rcopy(ref, ref, self.s.at[d - 1], self.r.at[d - 1], to).start()

        def _side(self, bb, i):
            ref = self.line(c, bb)
            rcopy(ref, ref, self.s.at[7 + i], self.r.at[7 + i], sibling).start()

        def second(self):
            for d in range(1, NS):
                got(self.block(c, b, mod(a - d, NS)), self.r.at[d - 1])
            ref = self.line(c, b)
            for i, d in enumerate((1, -1)):
                rcopy(ref, ref, self.s.at[3 + i], self.r.at[3 + i], place(c, mod(b + d, NS), a)).start()
            self._side(b, 0)

        def relay(self):
            for i, d in enumerate((1, -1)):
                bb = mod(b - d, NS)
                got(self.line(c, bb), self.r.at[3 + i])
                ref = self.half(c, bb, i)
                rcopy(ref, ref, self.s.at[5 + i], self.r.at[5 + i], place(c, mod(b + d, NS), a)).start()
                self._side(bb, 1 + i)

        def last(self):
            bb = mod(b + 2, NS)
            for i in range(2):
                got(self.half(c, bb, i), self.r.at[5 + i])
            self._side(bb, 3)

        def finish(self):
            for i, d in enumerate((0, -1, 1, 2)):
                got(self.line(1 - c, mod(a + d, NS)), self.r.at[7 + i])

        def drain(self):
            for i in range(3):
                sent(self.block(c, b, a), self.s.at[i])
            for i in range(2):
                sent(self.line(c, b), self.s.at[3 + i])
                sent(self.half(c, b, i), self.s.at[5 + i])
            for i in range(4):
                sent(self.line(c, b), self.s.at[7 + i])

    own_h = Gather(
        lambda cc, bb, aa: hown.at[cc, bb, aa],
        lambda cc, bb: hown.at[cc, bb],
        lambda cc, bb, i: hown.at[cc, bb, pl.ds(2 * i, 2)],
        h_sems,
    )
    def probs_gather(part, sems):
        rows = pl.ds(*PARTS[part])
        return Gather(
            lambda cc, bb, aa: pbuf.at[cc, bb, aa, rows],
            lambda cc, bb: pbuf.at[cc, bb, :, rows],
            lambda cc, bb, i: pbuf.at[cc, bb, pl.ds(2 * i, 2), rows],
            sems,
        )

    probs = [probs_gather(i, sems) for i, sems in enumerate((p_sems, q_sems, v_sems))]
    others = pl.ds(KEPT, ALL - KEPT)
    other_h = Gather(
        lambda cc, bb, aa: hall.at[cc, bb, aa, :, others],
        lambda cc, bb: hall.at[cc, bb, :, :, others],
        lambda cc, bb, i: hall.at[cc, bb, pl.ds(2 * i, 2), :, others],
        o_sems,
    )

    w_copy = pltpu.make_async_copy(w_hbm, w_ref, w_sem)
    w_copy.start()

    barrier = pltpu.get_barrier_semaphore()

    @pl.loop(1, NV)
    def _(d):
        pl.semaphore_signal(
            barrier, inc=1, device_id={"vocab": mod(me + d, NV)}, device_id_type=MESH
        )

    @pl.loop(1, NZ)
    def _(d):
        pl.semaphore_signal(barrier, inc=1, device_id=at_z(mod(z + d, NZ)), device_id_type=MESH)

    hown[c, b, a] = ht_ref[...]
    pbuf[c, b, a] = probs_ref[...]

    local = tiles_ref[...] - me * TILES
    local = jnp.where((local >= 0) & (local < TILES), local, 32)
    listed = lax.broadcasted_iota(jnp.int32, (NV, ROWS), 0) < count_ref[...]
    local = jnp.where(listed, local, -1).astype(F32).astype(BF16)
    slot = lax.shift_right_logical(lax.broadcasted_iota(jnp.int32, (NV, NV * RG), 1), 4)
    slot_b = lax.shift_right_logical(slot, 2) & 3
    slot_a = slot & 3
    position = jnp.where(slot < 16, slot_b * 8 + slot_a * 2, slot_a * 8 + slot_b * 2 + 1)
    spread = position == lax.broadcasted_iota(jnp.int32, (NV, NV * RG), 0)
    z_ref[...] = lax.dot_general(
        local, jnp.where(spread, 1.0, 0.0).astype(BF16), (((0,), (0,)), ((), ())),
        preferred_element_type=F32,
    )

    @pl.when(jnp.logical_not(owns3(z)))
    def _():
        t_in[2] = jnp.zeros((ALL, TILE), BF16)

    pl.semaphore_wait(barrier, NV - 1 + NZ - 1)

    for one in probs:
        one.first()
    own_h.first()
    for d in range(1, NZ):
        rcopy(
            hown.at[c, b, a], zin.at[NZ - d], zhs.at[d - 1], zhr.at[d - 1],
            at_z(mod(z + d, NZ)),
        ).start()
    for one in probs:
        one.second()
    own_h.second()
    for one in probs[:2]:
        one.relay()
    for d in range(1, NZ):
        got(zin.at[NZ - d], zhr.at[d - 1])
    hall[c, b, a] = jnp.concatenate([hown[c, b, a]] + [zin[d] for d in range(1, NZ)], axis=1)
    other_h.first()

    own = lax.rem(lax.broadcasted_iota(jnp.int32, (RG, NV * RG), 1), RG) == (
        lax.broadcasted_iota(jnp.int32, (RG, NV * RG), 0)
    )

    def place_rows(g):
        rows = pl.ds(pl.multiple_of(g * RG, RG), RG)
        spot = jnp.where(own, z_ref[rows, :], -1.0)
        blocks = [jnp.where(spot == float(n), 1.0, 0.0).astype(BF16) for n in range(TILES)]
        blocks.append(jnp.where(spot >= 0.0, 1.0, 0.0).astype(BF16))
        entries = pbuf[:, :, :, rows, :].reshape(NV * RG, TILE)
        placed = jnp.dot(jnp.concatenate(blocks, axis=0), entries, preferred_element_type=F32)
        for n in range(TILES):
            targ_ref[n, rows, :] = placed[n * RG : (n + 1) * RG].astype(BF16)
        mass_ref[rows, :] = placed[TILES * RG :]

    def build_part(part):
        low, size = PARTS[part]
        probs[part].last()
        probs[part].finish()
        pl.loop(low // RG, (low + size) // RG, unroll=2)(place_rows)

    def send_part(part):
        low, size = PARTS[part]
        rows = pl.ds(low, size)
        for d in (1, 7, 2, 6, 3, 5, 4):
            to = mod(z + d, NZ)
            there = pl.ds((NZ - d) * ROWS + low, size)
            for s in range(2):
                rcopy(
                    targ_ref.at[tile_of(to, s), rows], t_in.at[s, there], ts, tr, at_z(to)
                ).start()

            @pl.when(owns3(to))
            def _():
                rcopy(
                    targ_ref.at[tile_of(to, 2), rows], t_in.at[2, there],
                    ts2.at[d], tr2, at_z(to),
                ).start()

    build_part(0)
    send_part(0)
    probs[2].relay()
    own_h.relay()
    build_part(1)
    other_h.second()
    send_part(1)
    build_part(2)

    for s in range(2):
        t_in[s, 0:ROWS] = targ_ref[tile_of(z, s)]

    @pl.when(owns3(z))
    def _():
        t_in[2, 0:ROWS] = targ_ref[tile_of(z, 2)]

    own_h.last()
    own_h.finish()
    w_copy.wait()
    for i in range(NV // 2):
        yy, xx = i // NS, i % NS
        pair = jnp.concatenate([hown[0, yy, xx], hown[1, xx, yy]], axis=0)
        h_ref[:, i * 2 * BLK : (i + 1) * 2 * BLK] = pair.T

    peak = jnp.full((ROWS, TILE), -jnp.inf, F32)
    for lo, width in COLS:
        part = jnp.dot(h_ref[...], w_ref[:, lo : lo + width], preferred_element_type=F32)
        for t in range(width // TILE):
            one = part[:, t * TILE : (t + 1) * TILE]
            logit_ref[tile_rows(lo // TILE + t), :] = one
            peak = jnp.maximum(peak, one)
    peak = jnp.max(peak, axis=1, keepdims=True)
    mass = jnp.zeros((ROWS, TILE), F32)
    for t in range(TILES):
        mass = mass + jnp.exp(logit_ref[tile_rows(t), :] - peak)
    mass = jnp.sum(mass, axis=1, keepdims=True)

    lane = lax.broadcasted_iota(jnp.int32, (ROWS, TILE), 1)

    def message_of(first, second):
        packed = jnp.where(lane == 0, first, jnp.where(lane == 1, second, 0.0))
        packed = jnp.concatenate([packed, jnp.zeros((4 * TILE - ROWS, TILE), F32)], axis=0).T
        return jnp.concatenate(
            [packed[i : i + 1, k * TILE : (k + 1) * TILE] for i in range(2) for k in range(4)],
            axis=0,
        )

    message = message_of(peak, mass)
    stat_out[...] = message
    stat_in[me] = message

    @pl.loop(1, NV)
    def _(d):
        rcopy(stat_out, stat_in.at[me], st_s, st_r, {"vocab": mod(me + d, NV)}).start()

    for s in range(SLOTS):
        cols = tile_cols(tile_of(z, s))
        pieces = []
        for i in range(NV):
            cc, bb, aa = i // 16, i // 4 % 4, i % 4
            v = (bb * NS + aa) * NC if cc == 0 else (aa * NS + bb) * NC + 1
            pieces.append(w_ref[v * BLK : (v + 1) * BLK, cols])
        wt_ref[s * TILE : (s + 1) * TILE, :] = jnp.concatenate(pieces, axis=0).T

    teacher = jnp.sum(mass_ref[...], axis=1, keepdims=True)
    scale = 1.0 / teacher
    mass_ref[...] = jnp.broadcast_to(LOSS_SCALE * scale, (ROWS, TILE))
    scale_rows = message_of(LOSS_SCALE * scale, jnp.log(teacher))
    cross = jnp.zeros((ROWS, TILE), F32)
    for t in range(TILES):
        cross = cross + targ_ref[t].astype(F32) * logit_ref[tile_rows(t), :]
    entries = probs_ref[...].astype(F32)
    counts = jnp.broadcast_to(count_ref[...].astype(F32), (TILE, ROWS)).T
    weighted = jnp.where(counts > me.astype(F32), entries * jnp.log(entries), 0.0)
    shares = jnp.sum((weighted - cross) * scale)

    other_h.relay()
    send_part(2)

    got(stat_in.at[pl.ds(0, NV - 1)], st_r)
    stats = stat_in[...]
    peaks, masses = stats[:, 0:4, :], stats[:, 4:8, :]
    top = jnp.max(peaks, axis=0)
    real = (
        lax.broadcasted_iota(jnp.int32, (4, TILE), 0) * TILE
        + lax.broadcasted_iota(jnp.int32, (4, TILE), 1)
    ) < ROWS
    total = jnp.where(real, jnp.sum(masses * jnp.exp(peaks - top[None]), axis=0), 1.0)
    log_norm = jnp.where(real, top + jnp.log(total), 0.0)
    stat_z[0] = jnp.concatenate([log_norm, scale_rows[0:4]], axis=0)
    for d in range(1, NZ):
        rcopy(stat_z.at[0], stat_z.at[NZ - d], sz_s, sz_r, at_z(mod(z + d, NZ))).start()
    ln_ref[...] = to_all_lanes(log_norm)
    common = jnp.sum(jnp.where(real, log_norm - scale_rows[4:8], 0.0)) * (1.0 / NV)
    l1[me] = jnp.broadcast_to(shares + common, (8, TILE))

    @pl.loop(1, NV)
    def _(d):
        rcopy(l1.at[me], l1.at[me], l1s, l1r, {"vocab": mod(me + d, NV)}).start()

    @pl.loop(0, TILES)
    def _(t):
        soft = LOSS_SCALE * jnp.exp(logit_ref[tile_rows(t), :] - ln_ref[...])
        g_ref[:, tile_cols(t)] = (soft - targ_ref[t].astype(F32) * mass_ref[...]).astype(BF16)

    @pl.loop(0, 4)
    def _(i):
        rows = pl.ds(pl.multiple_of(i * 512, 512), 512)
        part = lax.dot_general(
            w_ref[rows, :], g_ref[...], (((1,), (1,)), ((), ())), preferred_element_type=F32
        )
        ghs[pl.ds(i * 8, 8)] = part.astype(BF16).reshape(8, BLK, ROWS)

    ghr[me] = ghs[me]
    hall[:, :, :, :, 0:KEPT] = hown[:, :, :, :, 0:KEPT]

    other_h.last()

    @pl.loop(1, NV)
    def _(d):
        to = mod(me + d, NV)
        rcopy(ghs.at[to], ghr.at[me], gh_s, gh_r, {"vocab": to}).start()

    got(l1.at[pl.ds(0, NV - 1)], l1r)
    l2[z] = jnp.sum(l1[...], axis=0)

    @pl.loop(1, NZ)
    def _(d):
        rcopy(l2.at[z], l2.at[z], l2s, l2r, at_z(mod(z + d, NZ))).start()

    got(stat_z.at[pl.ds(0, NZ - 1)], sz_r)
    lnf_ref[...] = jnp.concatenate(
        [flat_row(stat_z[d, 0:4])[:, :ROWS] for d in range(NZ)], axis=1
    )
    for d in range(NZ):
        col_ref[d * ROWS : (d + 1) * ROWS, :] = to_all_lanes(stat_z[d, 4:8])
    other_h.finish()

    @pl.loop(0, ALL // STEP)
    def _(k):
        lanes = pl.ds(pl.multiple_of(k * STEP, STEP), STEP)
        rows = hall[:, :, :, :, lanes].reshape(D, STEP)
        part = jnp.dot(wt_ref[...], rows, preferred_element_type=F32)
        soft = (LOSS_SCALE * jnp.exp(part - lnf_ref[:, lanes])).T
        for s in range(SLOTS):
            logit_ref[pl.ds(pl.multiple_of(s * ALL + k * STEP, STEP), STEP), :] = (
                soft[:, s * TILE : (s + 1) * TILE]
            )

    got(t_in.at[pl.ds(0, 2), pl.ds(ROWS, ALL - ROWS)], tr)

    @pl.when(owns3(z))
    def _():
        got(t_in.at[2, pl.ds(ROWS, ALL - ROWS)], tr2)

    @pl.loop(0, ALL // STEP)
    def _(k):
        rows = pl.ds(pl.multiple_of(k * STEP, STEP), STEP)
        for s in range(SLOTS):
            soft = logit_ref[pl.ds(pl.multiple_of(s * ALL + k * STEP, STEP), STEP), :]
            grad_ref[rows, s * TILE : (s + 1) * TILE] = (
                soft - t_in[s, rows, :].astype(F32) * col_ref[rows, :]
            ).astype(BF16)

    def head_block(j):
        yy, xx = lax.div(j, 2), 2 * lax.rem(j, 2)
        total = jnp.zeros((SLICE, WIDE), F32)
        for k in range(ALL // STEP):
            lanes = slice(k * STEP, (k + 1) * STEP)
            part = [
                hall[0, yy, xx, :, lanes], hall[1, xx, yy, :, lanes],
                hall[0, yy, xx + 1, :, lanes], hall[1, xx + 1, yy, :, lanes],
            ]
            total = total + jnp.dot(
                jnp.concatenate(part, axis=0), grad_ref[lanes, :], preferred_element_type=F32
            )
        return total.astype(BF16)

    @pl.loop(1, NZ)
    def _(i):
        j = mod(z + i, NZ)
        done = head_block(j)
        for s in range(SLOTS):
            gws[i, s] = done[:, s * TILE : (s + 1) * TILE]
        for s in range(2):
            rcopy(gws.at[i, s], gw_ref.at[:, tile_cols(tile_of(z, s))], ws, wr, at_z(j)).start()

        @pl.when(owns3(z))
        def _():
            rcopy(
                gws.at[i, 2], gw_ref.at[:, tile_cols(tile_of(z, 2))],
                ws2, wr2.at[lax.div(z, 3)], at_z(j),
            ).start()

    done = head_block(z)
    for s in range(2):
        gw_ref[:, tile_cols(tile_of(z, s))] = done[:, s * TILE : (s + 1) * TILE]

    @pl.when(owns3(z))
    def _():
        gw_ref[:, tile_cols(tile_of(z, 2))] = done[:, 2 * TILE :]

    got(ghr.at[pl.ds(0, NV - 1)], gh_r)
    sum_h = jnp.zeros((BLK, ROWS), F32)
    for i in range(NV):
        sum_h = sum_h + ghr[i].astype(F32)
    gh_ref[...] = sum_h.astype(BF16)
    got(l2.at[pl.ds(0, NZ - 1)], l2r)
    loss_ref[...] = jnp.sum(l2[...], axis=0) * (1.0 / (ROWS * NZ))

    for one in probs:
        one.drain()
    own_h.drain()
    other_h.drain()
    for d in range(1, NZ):
        sent(hown.at[c, b, a], zhs.at[d - 1])
    sent(stat_in.at[pl.ds(0, NV - 1)], st_s)
    sent(ghr.at[pl.ds(0, NV - 1)], gh_s)
    sent(l1.at[pl.ds(0, NV - 1)], l1s)
    sent(l2.at[pl.ds(0, NZ - 1)], l2s)
    sent(stat_z.at[pl.ds(0, NZ - 1)], sz_s)
    sent(t_in.at[pl.ds(0, 2), pl.ds(ROWS, ALL - ROWS)], ts)
    for d in range(1, NZ):

        @pl.when(owns3(mod(z + d, NZ)))
        def _():
            sent(targ_ref.at[0], ts2.at[d])

    sent(gws.at[pl.ds(1, NZ - 1), pl.ds(0, 2)], ws)

    @pl.when(owns3(z))
    def _():
        sent(gws.at[pl.ds(1, NZ - 1), 2], ws2)

    got(gws.at[pl.ds(1, NZ - 1), pl.ds(0, 2)], wr)
    for i in range(SLOTS):

        @pl.when(z != 3 * i)
        def _():
            got(gws.at[0, 0], wr2.at[i])


def shards(hidden, head_weight, kept_tiles, kept_count, teacher_probs):
    vmem = pl.BlockSpec(memory_space=pltpu.VMEM)
    dma = pltpu.SemaphoreType.DMA
    loss, gh, gw = pl.pallas_call(
        kernel,
        out_shape=(
            jax.ShapeDtypeStruct((8, TILE), F32),
            jax.ShapeDtypeStruct((BLK, ROWS), BF16),
            jax.ShapeDtypeStruct((SLICE, VOC), BF16),
        ),
        in_specs=[vmem, pl.BlockSpec(memory_space=pl.ANY), vmem, vmem, vmem],
        out_specs=(vmem, vmem, vmem),
        scratch_shapes=[
            pltpu.VMEM((D, VOC), BF16),
            pltpu.VMEM((NC, NS, NS, BLK, ALL), BF16),
            pltpu.VMEM((NC, NS, NS, BLK, ROWS), BF16),
            pltpu.VMEM((NZ, BLK, ROWS), BF16),
            pltpu.VMEM((1, ALL), F32),
            pltpu.VMEM((ALL, TILE), F32),
            pltpu.VMEM((ROWS, D), BF16),
            pltpu.VMEM((NC, NS, NS, ROWS, TILE), BF16),
            pltpu.VMEM((SLOTS * ALL, TILE), F32),
            pltpu.VMEM((TILES, ROWS, TILE), BF16),
            pltpu.VMEM((ROWS, VOC), BF16),
            pltpu.VMEM((ROWS, NV * RG), F32),
            pltpu.VMEM((ROWS, TILE), F32),
            pltpu.VMEM((ROWS, TILE), F32),
            pltpu.VMEM((WIDE, D), BF16),
            pltpu.VMEM((SLOTS, ALL, TILE), BF16),
            pltpu.VMEM((ALL, WIDE), BF16),
            pltpu.VMEM((NZ, SLOTS, SLICE, TILE), BF16),
            pltpu.VMEM((8, TILE), F32),
            pltpu.VMEM((NV, 8, TILE), F32),
            pltpu.VMEM((NZ, 8, TILE), F32),
            pltpu.VMEM((NV, BLK, ROWS), BF16),
            pltpu.VMEM((NV, BLK, ROWS), BF16),
            pltpu.VMEM((NV, 8, TILE), F32),
            pltpu.VMEM((NZ, 8, TILE), F32),
            dma, dma((NZ - 1,)), dma((NZ - 1,)),
            [dma((11,)), dma((11,))], [dma((11,)), dma((11,))], [dma((11,)), dma((11,))], [dma((11,)), dma((11,))], [dma((11,)), dma((11,))],
            dma, dma, dma, dma, dma, dma, dma, dma, dma, dma,
            dma, dma, dma((NZ,)), dma, dma, dma, dma, dma((SLOTS,)),
        ],
        compiler_params=pltpu.CompilerParams(
            collective_id=0, has_side_effects=True, vmem_limit_bytes=60 * 1024 * 1024
        ),
        cost_estimate=pl.CostEstimate(
            flops=8 * ROWS * D * VOC, bytes_accessed=2 * D * VOC, transcendentals=3 * ROWS * VOC
        ),
    )(
        hidden.T,
        head_weight,
        kept_tiles.T,
        kept_count.reshape(1, ROWS),
        teacher_probs.reshape(ROWS, TILE),
    )
    return loss[0, 0], gh.T, gw


def solution(mesh):
    return jax.shard_map(
        shards,
        mesh=mesh,
        in_specs=(
            P("dp", "vocab"),
            P(None, "vocab"),
            P("dp", None),
            P("dp"),
            P("dp", "vocab", None),
        ),
        out_specs=(P(), P("dp", "vocab"), P("dp", "vocab")),
        check_vma=False,
    )
```

```python
import jax
import jax.numpy as jnp
from jax import lax
from jax.experimental import pallas as pl
from jax.experimental.pallas import tpu as pltpu
from jax.sharding import PartitionSpec as P

LOSS_SCALE = 1024.0
MESH = pl.DeviceIdType.MESH
NS = 4
NC = 2
NV = NS * NS * NC
NZ = 8
ROWS = 448
D = 2048
BLK = D // NV
TILE = 128
VOC = 2432
TILES = VOC // TILE
SLOTS = 3
WIDE = SLOTS * TILE
SLICE = D // NZ
RG = 16
PARTS = ((0, 96), (96, 160), (256, 192))
ALL = ROWS * NZ
KEPT = 3 * TILE
STEP = 512
COLS = ((0, 512), (512, 512), (1024, 512), (1536, 512), (2048, 384))
F32 = jnp.float32
BF16 = jnp.bfloat16


def mod(a, n):
    return lax.rem(a + n, n)


def flat_row(rows4):
    return jnp.concatenate([rows4[a : a + 1, :] for a in range(4)], axis=1)


def to_all_lanes(rows4):
    return jnp.broadcast_to(flat_row(rows4), (TILE, 4 * TILE)).T[:ROWS, :]


def tile_cols(t):
    return pl.ds(pl.multiple_of(t * TILE, TILE), TILE)


def tile_rows(t):
    return slice(t * ROWS, (t + 1) * ROWS) if isinstance(t, int) else pl.ds(
        pl.multiple_of(t * ROWS, ROWS), ROWS
    )


def kernel(
    ht_ref, w_hbm, tiles_ref, count_ref, probs_ref,
    loss_ref, gh_ref, gw_ref,
    w_ref, hall, hown, zin, col_ref, h_ref, pbuf, logit_ref, targ_ref, g_ref, z_ref, mass_ref, ln_ref,
    wt_ref, t_in, grad_ref, gws, stat_out, stat_in, stat_z, ghs, ghr, l1, l2,
    w_sem, zhs, zhr, h_sems, p_sems, q_sems, v_sems, o_sems,
    st_s, st_r, gh_s, gh_r, l1s, l1r, l2s, l2r, sz_s, sz_r, ts, tr, ts2, tr2, ws, wr, ws2, wr2,
):
    me = lax.axis_index("vocab")
    z = lax.axis_index("dp")
    c = lax.rem(me, NC)
    chip = lax.div(me, NC)
    x = lax.rem(chip, NS)
    y = lax.div(chip, NS)
    a = x + c * (y - x)
    b = y + c * (x - y)

    def place(cc, bb, aa):
        yy = bb + cc * (aa - bb)
        xx = aa + cc * (bb - aa)
        return {"vocab": (yy * NS + xx) * NC + cc}

    sibling = {"vocab": chip * NC + 1 - c}

    def at_z(zz):
        return {"dp": zz}

    def owns3(zz):
        return lax.rem(zz, 3) == 0

    def tile_of(zz, s):
        return 16 + lax.div(zz, 3) if s == 2 else zz + 8 * s

    def rcopy(src, dst, ss, sr, dev):
        return pltpu.make_async_remote_copy(
            src_ref=src, dst_ref=dst, send_sem=ss, recv_sem=sr, device_id=dev, device_id_type=MESH
        )

    def got(ref, sem):
        rcopy(ref, ref, sem, sem, sibling).wait_recv()

    def sent(ref, sem):
        rcopy(ref, ref, sem, sem, sibling).wait_send()

    class Gather:
        def __init__(self, block, line, half, sems):
            self.block, self.line, self.half = block, line, half
            self.s, self.r = sems

        def first(self):
            for d in range(1, NS):
                ref = self.block(c, b, a)
                to = place(c, b, mod(a + d, NS))
                rcopy(ref, ref, self.s.at[d - 1], self.r.at[d - 1], to).start()

        def _side(self, bb, i):
            ref = self.line(c, bb)
            rcopy(ref, ref, self.s.at[7 + i], self.r.at[7 + i], sibling).start()

        def second(self):
            for d in range(1, NS):
                got(self.block(c, b, mod(a - d, NS)), self.r.at[d - 1])
            ref = self.line(c, b)
            for i, d in enumerate((1, -1)):
                rcopy(ref, ref, self.s.at[3 + i], self.r.at[3 + i], place(c, mod(b + d, NS), a)).start()
            self._side(b, 0)

        def relay(self):
            for i, d in enumerate((1, -1)):
                bb = mod(b - d, NS)
                got(self.line(c, bb), self.r.at[3 + i])
                ref = self.half(c, bb, i)
                rcopy(ref, ref, self.s.at[5 + i], self.r.at[5 + i], place(c, mod(b + d, NS), a)).start()
                self._side(bb, 1 + i)

        def last(self):
            bb = mod(b + 2, NS)
            for i in range(2):
                got(self.half(c, bb, i), self.r.at[5 + i])
            self._side(bb, 3)

        def finish(self):
            for i, d in enumerate((0, -1, 1, 2)):
                got(self.line(1 - c, mod(a + d, NS)), self.r.at[7 + i])

        def drain(self):
            for i in range(3):
                sent(self.block(c, b, a), self.s.at[i])
            for i in range(2):
                sent(self.line(c, b), self.s.at[3 + i])
                sent(self.half(c, b, i), self.s.at[5 + i])
            for i in range(4):
                sent(self.line(c, b), self.s.at[7 + i])

    own_h = Gather(
        lambda cc, bb, aa: hown.at[cc, bb, aa],
        lambda cc, bb: hown.at[cc, bb],
        lambda cc, bb, i: hown.at[cc, bb, pl.ds(2 * i, 2)],
        h_sems,
    )
    def probs_gather(part, sems):
        rows = pl.ds(*PARTS[part])
        return Gather(
            lambda cc, bb, aa: pbuf.at[cc, bb, aa, rows],
            lambda cc, bb: pbuf.at[cc, bb, :, rows],
            lambda cc, bb, i: pbuf.at[cc, bb, pl.ds(2 * i, 2), rows],
            sems,
        )

    probs = [probs_gather(i, sems) for i, sems in enumerate((p_sems, q_sems, v_sems))]
    others = pl.ds(KEPT, ALL - KEPT)
    other_h = Gather(
        lambda cc, bb, aa: hall.at[cc, bb, aa, :, others],
        lambda cc, bb: hall.at[cc, bb, :, :, others],
        lambda cc, bb, i: hall.at[cc, bb, pl.ds(2 * i, 2), :, others],
        o_sems,
    )

    w_copy = pltpu.make_async_copy(w_hbm, w_ref, w_sem)
    w_copy.start()

    barrier = pltpu.get_barrier_semaphore()

    @pl.loop(1, NV)
    def _(d):
        pl.semaphore_signal(
            barrier, inc=1, device_id={"vocab": mod(me + d, NV)}, device_id_type=MESH
        )

    @pl.loop(1, NZ)
    def _(d):
        pl.semaphore_signal(barrier, inc=1, device_id=at_z(mod(z + d, NZ)), device_id_type=MESH)

    hown[c, b, a] = ht_ref[...]
    pbuf[c, b, a] = probs_ref[...]

    local = tiles_ref[...] - me * TILES
    local = jnp.where((local >= 0) & (local < TILES), local, 32)
    listed = lax.broadcasted_iota(jnp.int32, (NV, ROWS), 0) < count_ref[...]
    local = jnp.where(listed, local, -1).astype(F32).astype(BF16)
    slot = lax.shift_right_logical(lax.broadcasted_iota(jnp.int32, (NV, NV * RG), 1), 4)
    slot_b = lax.shift_right_logical(slot, 2) & 3
    slot_a = slot & 3
    position = jnp.where(slot < 16, slot_b * 8 + slot_a * 2, slot_a * 8 + slot_b * 2 + 1)
    spread = position == lax.broadcasted_iota(jnp.int32, (NV, NV * RG), 0)
    z_ref[...] = lax.dot_general(
        local, jnp.where(spread, 1.0, 0.0).astype(BF16), (((0,), (0,)), ((), ())),
        preferred_element_type=F32,
    )

    @pl.when(jnp.logical_not(owns3(z)))
    def _():
        t_in[2] = jnp.zeros((ALL, TILE), BF16)

    pl.semaphore_wait(barrier, NV - 1 + NZ - 1)

    for one in probs:
        one.first()
    own_h.first()
    for d in range(1, NZ):
        rcopy(
            hown.at[c, b, a], zin.at[NZ - d], zhs.at[d - 1], zhr.at[d - 1],
            at_z(mod(z + d, NZ)),
        ).start()
    for one in probs:
        one.second()
    own_h.second()
    for one in probs[:2]:
        one.relay()
    for d in range(1, NZ):
        got(zin.at[NZ - d], zhr.at[d - 1])
    hall[c, b, a] = jnp.concatenate([hown[c, b, a]] + [zin[d] for d in range(1, NZ)], axis=1)
    other_h.first()

    own = lax.rem(lax.broadcasted_iota(jnp.int32, (RG, NV * RG), 1), RG) == (
        lax.broadcasted_iota(jnp.int32, (RG, NV * RG), 0)
    )

    def place_rows(g):
        rows = pl.ds(pl.multiple_of(g * RG, RG), RG)
        spot = jnp.where(own, z_ref[rows, :], -1.0)
        blocks = [jnp.where(spot == float(n), 1.0, 0.0).astype(BF16) for n in range(TILES)]
        blocks.append(jnp.where(spot >= 0.0, 1.0, 0.0).astype(BF16))
        entries = pbuf[:, :, :, rows, :].reshape(NV * RG, TILE)
        placed = jnp.dot(jnp.concatenate(blocks, axis=0), entries, preferred_element_type=F32)
        for n in range(TILES):
            targ_ref[n, rows, :] = placed[n * RG : (n + 1) * RG].astype(BF16)
        mass_ref[rows, :] = placed[TILES * RG :]

    def build_part(part):
        low, size = PARTS[part]
        probs[part].last()
        probs[part].finish()
        pl.loop(low // RG, (low + size) // RG, unroll=2)(place_rows)

    def send_part(part):
        low, size = PARTS[part]
        rows = pl.ds(low, size)
        for d in (1, 7, 2, 6, 3, 5, 4):
            to = mod(z + d, NZ)
            there = pl.ds((NZ - d) * ROWS + low, size)
            for s in range(2):
                rcopy(
                    targ_ref.at[tile_of(to, s), rows], t_in.at[s, there], ts, tr, at_z(to)
                ).start()

            @pl.when(owns3(to))
            def _():
                rcopy(
                    targ_ref.at[tile_of(to, 2), rows], t_in.at[2, there],
                    ts2.at[d], tr2, at_z(to),
                ).start()

    build_part(0)
    send_part(0)
    probs[2].relay()
    own_h.relay()
    build_part(1)
    other_h.second()
    send_part(1)
    build_part(2)

    for s in range(2):
        t_in[s, 0:ROWS] = targ_ref[tile_of(z, s)]

    @pl.when(owns3(z))
    def _():
        t_in[2, 0:ROWS] = targ_ref[tile_of(z, 2)]

    own_h.last()
    own_h.finish()
    w_copy.wait()
    for i in range(NV // 2):
        yy, xx = i // NS, i % NS
        pair = jnp.concatenate([hown[0, yy, xx], hown[1, xx, yy]], axis=0)
        h_ref[:, i * 2 * BLK : (i + 1) * 2 * BLK] = pair.T

    peak = jnp.full((ROWS, TILE), -jnp.inf, F32)
    for lo, width in COLS:
        part = jnp.dot(h_ref[...], w_ref[:, lo : lo + width], preferred_element_type=F32)
        for t in range(width // TILE):
            one = part[:, t * TILE : (t + 1) * TILE]
            logit_ref[tile_rows(lo // TILE + t), :] = one
            peak = jnp.maximum(peak, one)
    peak = jnp.max(peak, axis=1, keepdims=True)
    mass = jnp.zeros((ROWS, TILE), F32)
    for t in range(TILES):
        mass = mass + jnp.exp(logit_ref[tile_rows(t), :] - peak)
    mass = jnp.sum(mass, axis=1, keepdims=True)

    lane = lax.broadcasted_iota(jnp.int32, (ROWS, TILE), 1)

    def message_of(first, second):
        packed = jnp.where(lane == 0, first, jnp.where(lane == 1, second, 0.0))
        packed = jnp.concatenate([packed, jnp.zeros((4 * TILE - ROWS, TILE), F32)], axis=0).T
        return jnp.concatenate(
            [packed[i : i + 1, k * TILE : (k + 1) * TILE] for i in range(2) for k in range(4)],
            axis=0,
        )

    message = message_of(peak, mass)
    stat_out[...] = message
    stat_in[me] = message

    @pl.loop(1, NV)
    def _(d):
        rcopy(stat_out, stat_in.at[me], st_s, st_r, {"vocab": mod(me + d, NV)}).start()

    for s in range(SLOTS):
        cols = tile_cols(tile_of(z, s))
        pieces = []
        for i in range(NV):
            cc, bb, aa = i // 16, i // 4 % 4, i % 4
            v = (bb * NS + aa) * NC if cc == 0 else (aa * NS + bb) * NC + 1
            pieces.append(w_ref[v * BLK : (v + 1) * BLK, cols])
        wt_ref[s * TILE : (s + 1) * TILE, :] = jnp.concatenate(pieces, axis=0).T

    teacher = jnp.sum(mass_ref[...], axis=1, keepdims=True)
    scale = 1.0 / teacher
    mass_ref[...] = jnp.broadcast_to(LOSS_SCALE * scale, (ROWS, TILE))
    scale_rows = message_of(LOSS_SCALE * scale, jnp.log(teacher))
    cross = jnp.zeros((ROWS, TILE), F32)
    for t in range(TILES):
        cross = cross + targ_ref[t].astype(F32) * logit_ref[tile_rows(t), :]
    entries = probs_ref[...].astype(F32)
    counts = jnp.broadcast_to(count_ref[...].astype(F32), (TILE, ROWS)).T
    weighted = jnp.where(counts > me.astype(F32), entries * jnp.log(entries), 0.0)
    shares = jnp.sum((weighted - cross) * scale)

    other_h.relay()

    got(stat_in.at[pl.ds(0, NV - 1)], st_r)
    stats = stat_in[...]
    peaks, masses = stats[:, 0:4, :], stats[:, 4:8, :]
    top = jnp.max(peaks, axis=0)
    real = (
        lax.broadcasted_iota(jnp.int32, (4, TILE), 0) * TILE
        + lax.broadcasted_iota(jnp.int32, (4, TILE), 1)
    ) < ROWS
    total = jnp.where(real, jnp.sum(masses * jnp.exp(peaks - top[None]), axis=0), 1.0)
    log_norm = jnp.where(real, top + jnp.log(total), 0.0)
    stat_z[0] = jnp.concatenate([log_norm, scale_rows[0:4]], axis=0)
    for d in range(1, NZ):
        rcopy(stat_z.at[0], stat_z.at[NZ - d], sz_s, sz_r, at_z(mod(z + d, NZ))).start()
    send_part(2)
    ln_ref[...] = to_all_lanes(log_norm)
    common = jnp.sum(jnp.where(real, log_norm - scale_rows[4:8], 0.0)) * (1.0 / NV)
    l1[me] = jnp.broadcast_to(shares + common, (8, TILE))

    @pl.loop(1, NV)
    def _(d):
        rcopy(l1.at[me], l1.at[me], l1s, l1r, {"vocab": mod(me + d, NV)}).start()

    @pl.loop(0, TILES)
    def _(t):
        soft = LOSS_SCALE * jnp.exp(logit_ref[tile_rows(t), :] - ln_ref[...])
        g_ref[:, tile_cols(t)] = (soft - targ_ref[t].astype(F32) * mass_ref[...]).astype(BF16)

    @pl.loop(0, 4)
    def _(i):
        rows = pl.ds(pl.multiple_of(i * 512, 512), 512)
        part = lax.dot_general(
            w_ref[rows, :], g_ref[...], (((1,), (1,)), ((), ())), preferred_element_type=F32
        )
        ghs[pl.ds(i * 8, 8)] = part.astype(BF16).reshape(8, BLK, ROWS)

    ghr[me] = ghs[me]
    hall[:, :, :, :, 0:KEPT] = hown[:, :, :, :, 0:KEPT]

    other_h.last()

    @pl.loop(1, NV)
    def _(d):
        to = mod(me + d, NV)
        rcopy(ghs.at[to], ghr.at[me], gh_s, gh_r, {"vocab": to}).start()

    got(l1.at[pl.ds(0, NV - 1)], l1r)
    l2[z] = jnp.sum(l1[...], axis=0)

    @pl.loop(1, NZ)
    def _(d):
        rcopy(l2.at[z], l2.at[z], l2s, l2r, at_z(mod(z + d, NZ))).start()

    other_h.finish()

    @pl.loop(0, ALL // STEP)
    def _(k):
        lanes = pl.ds(pl.multiple_of(k * STEP, STEP), STEP)
        rows = hall[:, :, :, :, lanes].reshape(D, STEP)
        part = jnp.dot(wt_ref[...], rows, preferred_element_type=F32).T
        for s in range(SLOTS):
            logit_ref[pl.ds(pl.multiple_of(s * ALL + k * STEP, STEP), STEP), :] = (
                part[:, s * TILE : (s + 1) * TILE]
            )

    got(stat_z.at[pl.ds(0, NZ - 1)], sz_r)

    @pl.loop(0, NZ)
    def _(d):
        norm = to_all_lanes(stat_z[d, 0:4])
        col_ref[tile_rows(d), :] = to_all_lanes(stat_z[d, 4:8])
        for s in range(SLOTS):
            rows = tile_rows(s * NZ + d)
            logit_ref[rows, :] = LOSS_SCALE * jnp.exp(logit_ref[rows, :] - norm)

    got(t_in.at[pl.ds(0, 2), pl.ds(ROWS, ALL - ROWS)], tr)

    @pl.when(owns3(z))
    def _():
        got(t_in.at[2, pl.ds(ROWS, ALL - ROWS)], tr2)

    @pl.loop(0, ALL // STEP)
    def _(k):
        rows = pl.ds(pl.multiple_of(k * STEP, STEP), STEP)
        for s in range(SLOTS):
            soft = logit_ref[pl.ds(pl.multiple_of(s * ALL + k * STEP, STEP), STEP), :]
            grad_ref[rows, s * TILE : (s + 1) * TILE] = (
                soft - t_in[s, rows, :].astype(F32) * col_ref[rows, :]
            ).astype(BF16)

    def head_block(j):
        yy, xx = lax.div(j, 2), 2 * lax.rem(j, 2)
        total = jnp.zeros((SLICE, WIDE), F32)
        for k in range(ALL // STEP):
            lanes = slice(k * STEP, (k + 1) * STEP)
            part = [
                hall[0, yy, xx, :, lanes], hall[1, xx, yy, :, lanes],
                hall[0, yy, xx + 1, :, lanes], hall[1, xx + 1, yy, :, lanes],
            ]
            total = total + jnp.dot(
                jnp.concatenate(part, axis=0), grad_ref[lanes, :], preferred_element_type=F32
            )
        return total.astype(BF16)

    @pl.loop(1, NZ)
    def _(i):
        j = mod(z + i, NZ)
        done = head_block(j)
        for s in range(SLOTS):
            gws[i, s] = done[:, s * TILE : (s + 1) * TILE]
        for s in range(2):
            rcopy(gws.at[i, s], gw_ref.at[:, tile_cols(tile_of(z, s))], ws, wr, at_z(j)).start()

        @pl.when(owns3(z))
        def _():
            rcopy(
                gws.at[i, 2], gw_ref.at[:, tile_cols(tile_of(z, 2))],
                ws2, wr2.at[lax.div(z, 3)], at_z(j),
            ).start()

    done = head_block(z)
    for s in range(2):
        gw_ref[:, tile_cols(tile_of(z, s))] = done[:, s * TILE : (s + 1) * TILE]

    @pl.when(owns3(z))
    def _():
        gw_ref[:, tile_cols(tile_of(z, 2))] = done[:, 2 * TILE :]

    got(ghr.at[pl.ds(0, NV - 1)], gh_r)
    sum_h = jnp.zeros((BLK, ROWS), F32)
    for i in range(NV):
        sum_h = sum_h + ghr[i].astype(F32)
    gh_ref[...] = sum_h.astype(BF16)
    got(l2.at[pl.ds(0, NZ - 1)], l2r)
    loss_ref[...] = jnp.sum(l2[...], axis=0) * (1.0 / (ROWS * NZ))

    for one in probs:
        one.drain()
    own_h.drain()
    other_h.drain()
    for d in range(1, NZ):
        sent(hown.at[c, b, a], zhs.at[d - 1])
    sent(stat_in.at[pl.ds(0, NV - 1)], st_s)
    sent(ghr.at[pl.ds(0, NV - 1)], gh_s)
    sent(l1.at[pl.ds(0, NV - 1)], l1s)
    sent(l2.at[pl.ds(0, NZ - 1)], l2s)
    sent(stat_z.at[pl.ds(0, NZ - 1)], sz_s)
    sent(t_in.at[pl.ds(0, 2), pl.ds(ROWS, ALL - ROWS)], ts)
    for d in range(1, NZ):

        @pl.when(owns3(mod(z + d, NZ)))
        def _():
            sent(targ_ref.at[0], ts2.at[d])

    sent(gws.at[pl.ds(1, NZ - 1), pl.ds(0, 2)], ws)

    @pl.when(owns3(z))
    def _():
        sent(gws.at[pl.ds(1, NZ - 1), 2], ws2)

    got(gws.at[pl.ds(1, NZ - 1), pl.ds(0, 2)], wr)
    for i in range(SLOTS):

        @pl.when(z != 3 * i)
        def _():
            got(gws.at[0, 0], wr2.at[i])


def shards(hidden, head_weight, kept_tiles, kept_count, teacher_probs):
    vmem = pl.BlockSpec(memory_space=pltpu.VMEM)
    dma = pltpu.SemaphoreType.DMA
    loss, gh, gw = pl.pallas_call(
        kernel,
        out_shape=(
            jax.ShapeDtypeStruct((8, TILE), F32),
            jax.ShapeDtypeStruct((BLK, ROWS), BF16),
            jax.ShapeDtypeStruct((SLICE, VOC), BF16),
        ),
        in_specs=[vmem, pl.BlockSpec(memory_space=pl.ANY), vmem, vmem, vmem],
        out_specs=(vmem, vmem, vmem),
        scratch_shapes=[
            pltpu.VMEM((D, VOC), BF16),
            pltpu.VMEM((NC, NS, NS, BLK, ALL), BF16),
            pltpu.VMEM((NC, NS, NS, BLK, ROWS), BF16),
            pltpu.VMEM((NZ, BLK, ROWS), BF16),
            pltpu.VMEM((ALL, TILE), F32),
            pltpu.VMEM((ROWS, D), BF16),
            pltpu.VMEM((NC, NS, NS, ROWS, TILE), BF16),
            pltpu.VMEM((SLOTS * ALL, TILE), F32),
            pltpu.VMEM((TILES, ROWS, TILE), BF16),
            pltpu.VMEM((ROWS, VOC), BF16),
            pltpu.VMEM((ROWS, NV * RG), F32),
            pltpu.VMEM((ROWS, TILE), F32),
            pltpu.VMEM((ROWS, TILE), F32),
            pltpu.VMEM((WIDE, D), BF16),
            pltpu.VMEM((SLOTS, ALL, TILE), BF16),
            pltpu.VMEM((ALL, WIDE), BF16),
            pltpu.VMEM((NZ, SLOTS, SLICE, TILE), BF16),
            pltpu.VMEM((8, TILE), F32),
            pltpu.VMEM((NV, 8, TILE), F32),
            pltpu.VMEM((NZ, 8, TILE), F32),
            pltpu.VMEM((NV, BLK, ROWS), BF16),
            pltpu.VMEM((NV, BLK, ROWS), BF16),
            pltpu.VMEM((NV, 8, TILE), F32),
            pltpu.VMEM((NZ, 8, TILE), F32),
            dma, dma((NZ - 1,)), dma((NZ - 1,)),
            [dma((11,)), dma((11,))], [dma((11,)), dma((11,))], [dma((11,)), dma((11,))], [dma((11,)), dma((11,))], [dma((11,)), dma((11,))],
            dma, dma, dma, dma, dma, dma, dma, dma, dma, dma,
            dma, dma, dma((NZ,)), dma, dma, dma, dma, dma((SLOTS,)),
        ],
        compiler_params=pltpu.CompilerParams(
            collective_id=0, has_side_effects=True, vmem_limit_bytes=60 * 1024 * 1024
        ),
        cost_estimate=pl.CostEstimate(
            flops=8 * ROWS * D * VOC, bytes_accessed=2 * D * VOC, transcendentals=3 * ROWS * VOC
        ),
    )(
        hidden.T,
        head_weight,
        kept_tiles.T,
        kept_count.reshape(1, ROWS),
        teacher_probs.reshape(ROWS, TILE),
    )
    return loss[0, 0], gh.T, gw


def solution(mesh):
    return jax.shard_map(
        shards,
        mesh=mesh,
        in_specs=(
            P("dp", "vocab"),
            P(None, "vocab"),
            P("dp", None),
            P("dp"),
            P("dp", "vocab", None),
        ),
        out_specs=(P(), P("dp", "vocab"), P("dp", "vocab")),
        check_vma=False,
    )
```
